256 devices in a mesh: seq: 32 (over z, y), tp: 8 (over x, core).
Axes of the slice: x: 4, y: 4, z: 8, core: 2. Of those that a mesh axis runs over, the one named last changes fastest.
Arguments:
- tokens: bfloat16 [8192, 4096], P('seq', 'tp'), may hold values from -6 to 6
- w_query: bfloat16 [4096, 4096], P(None, 'tp'), may hold values from -0.09375 to 0.09375
- w_key: bfloat16 [4096, 1024], P(None, 'tp'), may hold values from -0.09375 to 0.09375
- w_value: bfloat16 [4096, 1024], P(None, 'tp'), may hold values from -0.09375 to 0.09375
- q_gain: float32 [128], replicated, may hold values from 0.1 to 1.9
- k_gain: float32 [128], replicated, may hold values from 0.1 to 1.9
- doc_lengths: int32 [16], replicated, may hold values from 1 to 4096, 8192 in all
- w_out: bfloat16 [4096, 4096], P('tp'), may hold values from -0.09375 to 0.09375
Outputs:
- mixed: bfloat16 [8192, 4096], P('seq', 'tp')
The draws below stay inside these ranges and needn't reach their ends.
Inputs may be any that keep to these rules, and one draw needn't show every extreme that they name: `doc_lengths`: whole numbers that sum to 8192; the largest is exactly 4096.
All inputs are finite; a program needn't handle non-finite values.
Results may differ from the reference program's by a relative error of at most 0.0073.
Values may be sent and summed in bfloat16 or wider, within the bound.
No kernel may reach another device: no remote copies, remote signals or barrier semaphores. Data moves between devices by JAX's collectives and lax.ppermute only.
A program may use at most 128 MiB of HBM per device.

```python
import math
import jax
import jax.numpy as jnp
import numpy as np
from jax import lax

D = 4096
QH = 32
KVH = 8
HD = 128
NDOCS = 16
TOKENS = 8192
MOST = 4096


def shard_levels(rng, dims, cuts, least, top_value):
    def one(dim, blocks):
        heights = jax.random.uniform(jax.random.fold_in(jax.random.fold_in(rng, 6), dim), (blocks,), jnp.float32, least / len(cuts), top_value / len(cuts))
        return jnp.repeat(jnp.exp(heights), dims[dim] // blocks).reshape((-1,) + (1,) * (len(dims) - dim - 1))

    level = one(*cuts[0])
    for cut in cuts[1:]:
        level = level * one(*cut)
    return level


def profile(count, total, reach, lean):
    portions = [(1 << 20) // math.isqrt(grade ** lean) + 1 for grade in range(2, count + 1)]
    spare, counts = total - reach - (count - 1), [1] * (count - 1)
    while spare > 0:
        movable = [i for i in range(count - 1) if counts[i] < reach]
        whole, left = sum([portions[i] for i in movable]), spare
        for i in movable:
            addition = min(reach - counts[i], max(1, left * portions[i] // whole), spare)
            counts[i] = counts[i] + addition
            spare = spare - addition
    return np.array([reach] + counts)


def ragged_sizes(stream_key, count, total, limit, lean):
    if count == 2:
        one = jax.random.randint(stream_key, (), max(1, total - limit), min(limit, total - 1) + 1)
        return jnp.stack([one, total - one])
    lengths = jnp.asarray(profile(count, total, limit, lean), jnp.int32)
    pairs = (count - 1) // 2
    donor, sink = lengths[1:1 + 2 * pairs:2], lengths[2:2 + 2 * pairs:2]
    margin = jnp.minimum(donor - 1, limit - sink)
    moved = jax.random.randint(jax.random.fold_in(stream_key, 1), (pairs,), 0, 1 << 20) % (margin + 1)
    lengths = lengths.at[1:1 + 2 * pairs:2].set(donor - moved).at[2:2 + 2 * pairs:2].set(sink + moved)
    return lengths[jax.random.permutation(jax.random.fold_in(stream_key, 2), count)]


def centred(stream_key, dims, scale, limit, split=(), kind=jnp.bfloat16):
    level = shard_levels(stream_key, dims, split, -0.22, 0.18) if split else 1.0
    entries = jax.random.normal(stream_key, dims, jnp.float32) * scale * level
    return jnp.minimum(jnp.maximum(entries, -limit), limit).astype(kind)


def setup_inputs(seed: int = 0) -> dict:
    key_list = jax.random.split(jax.random.key(seed), 9)
    return {
        "tokens": centred(key_list[0], (TOKENS, D), 1.0, 6.0, ((0, 32), (1, 8))),
        "w_query": centred(key_list[1], (D, QH * HD), D ** -0.5, 0.09375, ((1, 8),)),
        "w_key": centred(key_list[2], (D, KVH * HD), D ** -0.5, 0.09375, ((1, 8),)),
        "w_value": centred(key_list[3], (D, KVH * HD), D ** -0.5, 0.09375, ((1, 8),)),
        "q_gain": jnp.clip(1.0 + 0.18 * jax.random.normal(key_list[4], (HD,), jnp.float32), 0.1, 1.9),
        "k_gain": jnp.clip(1.0 + 0.18 * jax.random.normal(key_list[5], (HD,), jnp.float32), 0.1, 1.9),
        "doc_lengths": ragged_sizes(key_list[6], NDOCS, TOKENS, MOST, 2).astype(jnp.int32),
        "w_out": centred(key_list[7], (QH * HD, D), (QH * HD) ** -0.5, 0.09375, ((0, 8),)),
    }


EPSILON = 1e-06
ROPE_THETA = 1000000.0

def doc_tables(doc_lengths, token_index):
    doc_ends = jnp.cumsum(doc_lengths).astype(jnp.int32)
    passed = (token_index[:, None] >= doc_ends[None, :]).astype(jnp.int32)
    segment = lax.optimization_barrier(jnp.sum(passed, axis=1)).astype(jnp.int32)
    doc_start = lax.optimization_barrier(jnp.sum(passed * doc_lengths[None, :], axis=1)).astype(jnp.int32)
    return (segment, token_index - doc_start)

def rope_tables(position, head_width):
    half_width = head_width // 2
    frequency = ROPE_THETA ** (-(jnp.arange(half_width, dtype=jnp.float32) * 2.0 / head_width))
    angles = position.astype(jnp.float32)[:, None] * frequency[None, :]
    return (jnp.cos(angles), jnp.sin(angles))

def norm_rotate(inputs_f, gain, cosine, sine_part):
    inv_scale = lax.rsqrt(lax.optimization_barrier(jnp.mean(inputs_f * inputs_f, axis=-1, keepdims=True)) + EPSILON)
    scaled = inputs_f * inv_scale * gain
    half_width = scaled.shape[-1] // 2
    lower_half = scaled[..., :half_width]
    upper_half = scaled[..., half_width:]
    cos_wide = cosine[:, None, :]
    sin_wide = sine_part[:, None, :]
    return jnp.concatenate([lower_half * cos_wide - upper_half * sin_wide, upper_half * cos_wide + lower_half * sin_wide], axis=-1)

def attend(queries, query_seg, query_idx, keys_head, values_head, key_seg, key_idx, head_width):
    row_count = queries.shape[0]
    block_rows = min(512, row_count)
    query_blocks = queries.reshape(row_count // block_rows, block_rows, head_width)
    seg_blocks = query_seg.reshape(row_count // block_rows, block_rows)
    idx_blocks = query_idx.reshape(row_count // block_rows, block_rows)

    def block_attend(members):
        query_block, seg_block, idx_block = members
        scores = lax.dot_general(query_block, keys_head, (((1,), (1,)), ((), ())), preferred_element_type=jnp.float32)
        scores = scores / jnp.sqrt(jnp.float32(head_width))
        keep = (seg_block[:, None] == key_seg[None, :]) & (key_idx[None, :] <= idx_block[:, None])
        scores = jnp.where(keep, scores, jnp.float32(-1e+30))
        row_max = lax.optimization_barrier(jnp.max(scores, axis=1, keepdims=True))
        weights = jnp.exp(scores - row_max)
        row_sum = lax.optimization_barrier(jnp.sum(weights, axis=1, keepdims=True))
        weights_bf = (weights / row_sum).astype(jnp.bfloat16)
        return jnp.dot(weights_bf, values_head, preferred_element_type=jnp.float32).astype(jnp.bfloat16)
    attended = lax.map(block_attend, (query_blocks, seg_blocks, idx_blocks))
    return attended.reshape(row_count, head_width)

def reference(tokens, w_query, w_key, w_value, q_gain, k_gain, doc_lengths, w_out):
    token_index = jnp.arange(TOKENS, dtype=jnp.int32)
    segment, position = doc_tables(doc_lengths, token_index)
    cosine, sine_part = rope_tables(position, HD)
    queries = jnp.dot(tokens, w_query, preferred_element_type=jnp.float32).reshape(TOKENS, QH, HD)
    queries = norm_rotate(queries, q_gain, cosine, sine_part).astype(jnp.bfloat16)
    keys_all = jnp.dot(tokens, w_key, preferred_element_type=jnp.float32).reshape(TOKENS, KVH, HD)
    keys_all = norm_rotate(keys_all, k_gain, cosine, sine_part).astype(jnp.bfloat16)
    values_all = jnp.dot(tokens, w_value, preferred_element_type=jnp.float32).astype(jnp.bfloat16).reshape(TOKENS, KVH, HD)
    group_size = QH // KVH

    def one_head(head_number):
        kv_number = head_number // group_size
        query_head = lax.dynamic_index_in_dim(queries, head_number, 1, keepdims=False)
        keys_head = lax.dynamic_index_in_dim(keys_all, kv_number, 1, keepdims=False)
        values_head = lax.dynamic_index_in_dim(values_all, kv_number, 1, keepdims=False)
        return attend(query_head, segment, token_index, keys_head, values_head, segment, token_index, HD)
    heads_out = lax.map(one_head, jnp.arange(QH, dtype=jnp.int32))
    attended = jnp.transpose(heads_out, (1, 0, 2)).reshape(TOKENS, QH * HD)
    return jnp.dot(attended, w_out, preferred_element_type=jnp.float32).astype(jnp.bfloat16)
```

```python
import functools
import math

import jax
import jax.numpy as jnp
from jax import lax
from jax.experimental import pallas as pl
from jax.experimental.pallas import tpu as pltpu
from jax.sharding import PartitionSpec as P

EPSILON = 1e-06
ROPE_THETA = 1000000.0
BF = jnp.bfloat16
F32 = jnp.float32
VMEM = pltpu.VMEM
VLIMIT = 48 * 1024 * 1024


def params():
    return pltpu.CompilerParams(vmem_limit_bytes=VLIMIT)


def doc_tables(doc_lengths, token_index):
    doc_ends = jnp.cumsum(doc_lengths)
    passed = (token_index[:, None] >= doc_ends[None, :]).astype(jnp.int32)
    return jnp.sum(passed * doc_lengths[None, :], axis=1)


def rope_tables(position, head_width):
    half = head_width // 2
    frequency = ROPE_THETA ** (-(jnp.arange(half, dtype=F32) * 2.0 / head_width))
    angles = position.astype(F32)[:, None] * frequency[None, :]
    cos, sin = jnp.cos(angles), jnp.sin(angles)
    return jnp.concatenate([cos, cos], axis=1), jnp.concatenate([-sin, sin], axis=1)


def project_kernel(count, order, *refs):
    chunks = refs[:count]
    wq, wk, wv = refs[count : count + 3]
    rest = refs[count + 3 :]
    step = pl.program_id(0)

    def add(chunk, acc, first):
        x = chunk[...]
        nq = wq.shape[1]
        nk = wk.shape[1]
        parts = (
            (slice(0, nq), wq),
            (slice(nq, nq + nk), wk),
            (slice(nq + nk, nq + 2 * nk), wv),
        )
        for cols, w in parts:
            prod = jnp.dot(x, w[...], preferred_element_type=F32)
            acc[:, cols] = prod if first else acc[:, cols] + prod

    return chunks, wq, wk, wv, rest, step, add


def project_first(count, order, *refs):
    chunks, wq, wk, wv, rest, step, add = project_kernel(count, order, *refs)
    (acc,) = rest
    for k in range(count):

        @pl.when(step == k)
        def _(k=k):
            add(chunks[k], acc, k == 0)


def project_last(count, head, order, *refs):
    chunks, wq, wk, wv, rest, step, add = project_kernel(count, order, *refs)
    acc_in, cos_ref, sin_ref, qg, kg, q_out, kv_out, acc = rest

    @pl.when(step == 0)
    def _():
        acc[...] = acc_in[...]

    for k in range(count):

        @pl.when(step == k)
        def _(k=k):
            add(chunks[k], acc, False)

    @pl.when(step == count - 1)
    def _():
        rows = acc.shape[0]
        cos = cos_ref[...]
        sin = sin_ref[...]
        heads = wq.shape[1] // head

        def norm_rotate(x, gain):
            inv = lax.rsqrt(jnp.mean(x * x, axis=-1, keepdims=True) + EPSILON)
            x = x * inv * gain
            return (x * cos + pltpu.roll(x, head // 2, 1) * sin).astype(BF)

        kcol = heads * head
        kv_out[:, :head] = norm_rotate(acc[:, kcol : kcol + head], kg[...])
        kv_out[:, head:] = acc[:, kcol + head : kcol + 2 * head].astype(BF)
        for h in range(heads):
            q_out[h * rows : (h + 1) * rows, :] = norm_rotate(
                acc[:, h * head : (h + 1) * head], qg[...]
            )


def whole(shape):
    return pl.BlockSpec(shape, lambda *a: (0,) * len(shape))


def project(chunks, order, w_query, w_key, w_value, last=None):
    count = len(chunks)
    rows, depth = chunks[0].shape
    nq, nk = w_query.shape[1], w_key.shape[1]
    width = nq + 2 * nk
    specs = [whole((rows, depth))] * count + [
        pl.BlockSpec((depth, n), lambda k, idx: (idx[k], 0)) for n in (nq, nk, nk)
    ]
    cost = pl.CostEstimate(
        flops=2 * rows * depth * count * width,
        bytes_accessed=2 * depth * count * (width + rows) + 4 * rows * width,
        transcendentals=0,
    )
    if last is None:
        return pl.pallas_call(
            functools.partial(project_first, count),
            grid_spec=pltpu.PrefetchScalarGridSpec(
                num_scalar_prefetch=1,
                grid=(count,),
                in_specs=specs,
                out_specs=whole((rows, width)),
            ),
            out_shape=jax.ShapeDtypeStruct((rows, width), F32),
            compiler_params=params(),
            cost_estimate=cost,
            name="project_first",
        )(order, *chunks, w_query, w_key, w_value)
    acc, cos, sin, qg, kg = last
    head = cos.shape[1]
    specs += [whole((rows, width)), whole(cos.shape), whole(sin.shape), whole((1, head)), whole((1, head))]
    heads = nq // head
    return pl.pallas_call(
        functools.partial(project_last, count, head),
        grid_spec=pltpu.PrefetchScalarGridSpec(
            num_scalar_prefetch=1,
            grid=(count,),
            in_specs=specs,
            out_specs=[whole((heads * rows, head)), whole((rows, 2 * head))],
            scratch_shapes=[pltpu.VMEM((rows, width), F32)],
        ),
        out_shape=[
            jax.ShapeDtypeStruct((heads * rows, head), BF),
            jax.ShapeDtypeStruct((rows, 2 * head), BF),
        ],
        compiler_params=params(),
        cost_estimate=cost,
        name="project_last",
    )(order, *chunks, w_query, w_key, w_value, acc, cos, sin, qg, kg)


def attend_kernel(layout, first, final, scal, *refs):
    n = len(layout)
    q_ref, start_ref, index_ref = refs[:3]
    kvs = refs[3 : 3 + n]
    rest = refs[3 + n :]
    if first:
        out, acc = rest
    else:
        acc_in, out, acc = rest
    rows, head = q_ref.shape
    tok = start_ref.shape[0]
    heads = rows // tok
    scale = math.log2(math.e) / math.sqrt(head)
    acc[...] = jnp.zeros_like(acc) if first else acc_in[...]
    own, least, largest = scal[0], scal[1], scal[2]
    ones = jnp.ones((tok, head), BF)

    def block(kv, at, base, masked):
        keys = kv[at : at + tok, :head]
        values = jnp.concatenate([kv[at : at + tok, head:], ones], axis=1)
        if masked:
            col = base + lax.broadcasted_iota(jnp.int32, (tok, tok), 1)
            keep = (col >= start_ref[...]) & (col <= index_ref[...])
        for h in range(heads):
            part = slice(h * tok, (h + 1) * tok)
            s = lax.dot_general(
                q_ref[part, :], keys, (((1,), (1,)), ((), ())), preferred_element_type=F32
            )
            p = jnp.exp2(s * scale)
            if masked:
                p = jnp.where(keep, p, 0.0)
            acc[part, :] += jnp.dot(p.astype(BF), values, preferred_element_type=F32)

    at_block = 0
    for kv, count in zip(kvs, layout):
        for j in range(count):
            base = scal[3 + at_block]
            at_block += 1
            needed = (base + tok > least) & (base <= own)
            full = (base >= largest) & (base < own)
            pl.when(needed & full)(functools.partial(block, kv, j * tok, base, False))
            pl.when(needed & jnp.logical_not(full))(
                functools.partial(block, kv, j * tok, base, True)
            )
    if final:
        for h in range(heads):
            part = slice(h * tok, (h + 1) * tok)
            out[:, h * head : (h + 1) * head] = (acc[part, :head] / acc[part, head:]).astype(BF)
    else:
        out[...] = acc[...]


def attend(scal, q, start, index, kvs, acc=None, final=False):
    rows, head = q.shape
    tok = start.shape[0]
    layout = tuple(kv.shape[0] // tok for kv in kvs)
    first = acc is None
    args = [q, start, index, *kvs] + ([] if first else [acc])
    if final:
        shape = jax.ShapeDtypeStruct((tok, rows // tok * head), BF)
    else:
        shape = jax.ShapeDtypeStruct((rows, 2 * head), F32)
    blocks = sum(layout)
    return pl.pallas_call(
        functools.partial(attend_kernel, layout, first, final),
        in_specs=[pl.BlockSpec(memory_space=pltpu.SMEM)]
        + [pl.BlockSpec(memory_space=VMEM)] * len(args),
        out_specs=pl.BlockSpec(memory_space=VMEM),
        out_shape=shape,
        scratch_shapes=[pltpu.VMEM((rows, 2 * head), F32)],
        compiler_params=params(),
        cost_estimate=pl.CostEstimate(
            flops=blocks * rows * tok * head * 4,
            bytes_accessed=rows * head * 16,
            transcendentals=blocks * rows * tok,
        ),
        name="attend",
    )(scal, *args)


def out_kernel(idx, a_ref, b_ref, wa_ref, wb_ref, out):
    s = jnp.dot(a_ref[...], wa_ref[...], preferred_element_type=F32)
    s += jnp.dot(b_ref[...], wb_ref[...], preferred_element_type=F32)
    out[...] = s.astype(out.dtype)


def out_project(idx, a, b, w_own, w_sib, kind):
    rows, depth = a.shape
    cols = w_sib.shape[1] // 4
    return pl.pallas_call(
        out_kernel,
        grid_spec=pltpu.PrefetchScalarGridSpec(
            num_scalar_prefetch=1,
            grid=(1,),
            in_specs=[
                whole((rows, depth)),
                whole((rows, depth)),
                pl.BlockSpec((depth, cols), lambda i, idx: (0, idx[0])),
                pl.BlockSpec((depth, cols), lambda i, idx: (0, idx[1])),
            ],
            out_specs=whole((rows, cols)),
        ),
        out_shape=jax.ShapeDtypeStruct((rows, cols), kind),
        compiler_params=params(),
        cost_estimate=pl.CostEstimate(
            flops=4 * rows * depth * cols,
            bytes_accessed=4 * depth * cols + 4 * rows * depth,
            transcendentals=0,
        ),
        name="out_project",
    )(idx, a, b, w_own, w_sib)


def on_device(tokens, w_query, w_key, w_value, q_gain, k_gain, doc_lengths, w_out):
    tok, part = tokens.shape
    head = q_gain.shape[0]
    seqs, tps = lax.axis_size("seq"), lax.axis_size("tp")
    ny = 4
    nz = seqs // ny
    nx = tps // 2
    my_seq = lax.axis_index("seq")
    my_tp = lax.axis_index("tp")
    zi, yi = my_seq // ny, my_seq % ny
    xi, ci = my_tp // 2, my_tp % 2
    turn = 1 - 2 * ci

    def sibling(a):
        return lax.ppermute(a, "tp", [(i, i ^ 1) for i in range(tps)])

    def along_x(a, d):
        return lax.ppermute(
            a,
            "tp",
            [(i, (i // 2 + (d if i % 2 == 0 else -d)) % nx * 2 + i % 2) for i in range(tps)],
        )

    def along_y(a, d):
        return lax.ppermute(a, "seq", [(i, i // ny * ny + (i + d) % ny) for i in range(seqs)])

    def along_z(a, d):
        return lax.ppermute(a, "seq", [(i, (i // ny + d) % nz * ny + i % ny) for i in range(seqs)])

    own = tokens
    a1, a3, a2 = along_x(own, 1), along_x(own, nx - 1), along_x(own, 2)
    b0 = sibling(own)
    b1, b3, b2 = sibling(a1), sibling(a3), sibling(a2)
    low, high = (xi - turn) % nx, (xi + turn) % nx
    far = (xi + 2) % nx
    sc = 1 - ci
    order_first = jnp.stack(
        [2 * xi + ci, 2 * xi + sc, 2 * low + ci, 2 * high + ci, 2 * high + sc, 2 * low + sc]
    ).astype(jnp.int32)
    order_last = jnp.stack([2 * far + ci, 2 * far + sc]).astype(jnp.int32)

    token_index = my_seq * tok + jnp.arange(tok, dtype=jnp.int32)
    start = doc_tables(doc_lengths, token_index)
    cos, sin = rope_tables(token_index - start, head)

    acc = project([own, b0, a1, a3, b1, b3], order_first, w_query, w_key, w_value)
    queries, kv = project(
        [a2, b2],
        order_last,
        w_query,
        w_key,
        w_value,
        last=(acc, cos, sin, q_gain[None, :], k_gain[None, :]),
    )

    cols = w_out.shape[1] // tps
    w_out_late, kv = lax.optimization_barrier((w_out, kv))
    pairs = w_out_late.reshape(w_out.shape[0], nx, 2, cols)
    w_send = lax.dynamic_index_in_dim(pairs, sc, 2, keepdims=False).reshape(w_out.shape[0], nx * cols)
    w_sib = sibling(w_send)

    r1 = along_z(kv, 1)
    r2 = along_z(kv, 2)
    m2 = along_z(kv, -2)
    near = jnp.concatenate([r1, r2], axis=0)
    near_y = [along_y(near, e) for e in (1, 3, 2)]
    r3 = along_z(r1, 2)
    r4 = along_z(m2, -2)
    far_y = [
        along_y(jnp.concatenate([r3, jnp.where(yi + e < ny, kv, r4)], axis=0), e) for e in (1, 3, 2)
    ]

    def base(k, e):
        return ((zi - k) * ny + (yi - e) % ny) * tok

    def mixed_base(e):
        return (zi * ny + yi - e - jnp.where(yi < e, 3 * ny, 0)) * tok

    head_scal = [my_seq * tok, start[0], start[-1]]

    def scalars(bases):
        return jnp.stack(head_scal + bases).astype(jnp.int32)

    start_col, index_col = start[:, None], token_index[:, None]
    o = attend(
        scalars([base(0, 0), base(1, 0), base(2, 0)]), queries, start_col, index_col, [kv, r1, r2]
    )
    o = attend(
        scalars([base(k, e) for e in (1, 3, 2) for k in (1, 2)]),
        queries, start_col, index_col, near_y, o,
    )
    attended = attend(
        scalars(
            [base(3, 0), base(4, 0)] + [b for e in (1, 3, 2) for b in (base(3, e), mixed_base(e))]
        ),
        queries, start_col, index_col, [r3, r4] + far_y, o, final=True,
    )

    attended_sib = sibling(attended)

    def partial(target, kind=BF):
        idx = jnp.stack([2 * target + ci, target]).astype(jnp.int32)
        return out_project(idx, attended, attended_sib, w_out, w_sib, kind)

    t2 = along_x(partial(far), 2)
    t1 = along_x(partial(high), 1)
    t3 = along_x(partial(low), nx - 1)
    mine = partial(xi, F32)
    total = mine + t1.astype(F32) + t2.astype(F32) + t3.astype(F32)
    return total.astype(BF)


def solution(mesh):
    return jax.shard_map(
        on_device,
        mesh=mesh,
        in_specs=(
            P("seq", "tp"),
            P(None, "tp"),
            P(None, "tp"),
            P(None, "tp"),
            P(),
            P(),
            P(),
            P("tp", None),
        ),
        out_specs=P("seq", "tp"),
        check_vma=False,
    )
```

```python
import functools
import math

import jax
import jax.numpy as jnp
from jax import lax
from jax.experimental import pallas as pl
from jax.experimental.pallas import tpu as pltpu
from jax.sharding import PartitionSpec as P

EPSILON = 1e-06
ROPE_THETA = 1000000.0
BF = jnp.bfloat16
F32 = jnp.float32
VMEM = pltpu.VMEM
VLIMIT = 24 * 1024 * 1024


def params():
    return pltpu.CompilerParams(vmem_limit_bytes=VLIMIT)


def doc_tables(doc_lengths, token_index):
    doc_ends = jnp.cumsum(doc_lengths)
    passed = (token_index[:, None] >= doc_ends[None, :]).astype(jnp.int32)
    return jnp.sum(passed * doc_lengths[None, :], axis=1)


def rope_tables(position, head_width):
    half = head_width // 2
    frequency = ROPE_THETA ** (-(jnp.arange(half, dtype=F32) * 2.0 / head_width))
    angles = position.astype(F32)[:, None] * frequency[None, :]
    cos, sin = jnp.cos(angles), jnp.sin(angles)
    return jnp.concatenate([cos, cos], axis=1), jnp.concatenate([-sin, sin], axis=1)


def stage_kernel(plan, sources, idx, *refs):
    ins, rest = refs[:sources], refs[sources:]
    outs, sem = rest[:-1], rest[-1]
    copies = []
    for n, (src, axis, size, at, dst, row, col, cols) in enumerate(plan):
        cut = pl.ds(pl.multiple_of(idx[at] * size, size), size)
        view = ins[src].at[cut, :] if axis == 0 else ins[src].at[:, cut]
        copies.append(
            pltpu.make_async_copy(view, outs[dst].at[row, :, col : col + cols], sem.at[n])
        )
    for c in copies:
        c.start()
    for c in copies:
        c.wait()


def stage(idx, arrays, plan, shapes, name):
    return pl.pallas_call(
        functools.partial(stage_kernel, plan, len(arrays)),
        in_specs=[pl.BlockSpec(memory_space=pltpu.SMEM)]
        + [pl.BlockSpec(memory_space=pltpu.HBM)] * len(arrays),
        out_specs=[pl.BlockSpec(memory_space=VMEM)] * len(shapes),
        out_shape=[jax.ShapeDtypeStruct(shape, BF) for shape in shapes],
        scratch_shapes=[pltpu.SemaphoreType.DMA((len(plan),))],
        compiler_params=params(),
        cost_estimate=pl.CostEstimate(
            flops=0, bytes_accessed=sum(4 * math.prod(shape) for shape in shapes), transcendentals=0
        ),
        name=name,
    )(idx, *arrays)


def project_kernel(count, at, head, first, last, *refs):
    chunks, w = refs[:count], refs[count]
    rest = refs[count + 1 :]
    total = None
    for k in range(count):
        prod = jnp.dot(chunks[k][...], w[at + k], preferred_element_type=F32)
        total = prod if total is None else total + prod
    if not first:
        total = total + rest[0][...]
        rest = rest[1:]
    if not last:
        rest[0][...] = total
        return
    cos_ref, sin_ref, qg, kg, q_out, kv_out = rest
    cos = cos_ref[...]
    sin = sin_ref[...]
    rows = total.shape[0]
    heads = total.shape[1] // head - 2

    def norm_rotate(x, gain):
        inv = lax.rsqrt(jnp.mean(x * x, axis=-1, keepdims=True) + EPSILON)
        x = x * inv * gain
        return (x * cos + pltpu.roll(x, head // 2, 1) * sin).astype(BF)

    kcol = heads * head
    kv_out[:, :head] = norm_rotate(total[:, kcol : kcol + head], kg[...])
    kv_out[:, head:] = total[:, kcol + head : kcol + 2 * head].astype(BF)
    for h in range(heads):
        q_out[h * rows : (h + 1) * rows, :] = norm_rotate(
            total[:, h * head : (h + 1) * head], qg[...]
        )


def project(chunks, w, at, acc=None, last=None):
    count = len(chunks)
    rows, depth = chunks[0].shape
    width = w.shape[2]
    args = [*chunks, w] + ([] if acc is None else [acc]) + (list(last) if last else [])
    head = last[0].shape[1] if last else 128
    if last:
        heads = width // head - 2
        shape = [
            jax.ShapeDtypeStruct((heads * rows, head), BF),
            jax.ShapeDtypeStruct((rows, 2 * head), BF),
        ]
    else:
        shape = jax.ShapeDtypeStruct((rows, width), F32)
    vm = pl.BlockSpec(memory_space=VMEM)
    return pl.pallas_call(
        functools.partial(project_kernel, count, at, head, acc is None, last is not None),
        in_specs=[vm] * len(args),
        out_specs=[vm, vm] if last else vm,
        out_shape=shape,
        compiler_params=params(),
        cost_estimate=pl.CostEstimate(
            flops=4 * rows * depth * count * width,
            bytes_accessed=2 * depth * count * width,
            transcendentals=0,
        ),
        name="project",
    )(*args)


def attend_kernel(layout, at_block, first, final, scal, *refs):
    n = len(layout)
    q_ref, start_ref, index_ref = refs[:3]
    kvs = refs[3 : 3 + n]
    rest = refs[3 + n :]
    if first:
        out, acc = rest
    else:
        acc_in, out, acc = rest
    rows, head = q_ref.shape
    tok = start_ref.shape[0]
    heads = rows // tok
    scale = math.log2(math.e) / math.sqrt(head)
    acc[...] = jnp.zeros_like(acc) if first else acc_in[...]
    own, least, largest = scal[0], scal[1], scal[2]
    ones = jnp.ones((tok, head), BF)

    def block(kv, at, base, masked):
        keys = kv[at : at + tok, :head]
        values = jnp.concatenate([kv[at : at + tok, head:], ones], axis=1)
        if masked:
            col = base + lax.broadcasted_iota(jnp.int32, (tok, tok), 1)
            keep = (col >= start_ref[...]) & (col <= index_ref[...])
        for h in range(heads):
            part = slice(h * tok, (h + 1) * tok)
            s = lax.dot_general(
                q_ref[part, :], keys, (((1,), (1,)), ((), ())), preferred_element_type=F32
            )
            p = jnp.exp2(s * scale)
            if masked:
                p = jnp.where(keep, p, 0.0)
            acc[part, :] += jnp.dot(p.astype(BF), values, preferred_element_type=F32)

    for kv, count in zip(kvs, layout):
        for j in range(count):
            base = scal[3 + at_block]
            at_block += 1
            needed = (base + tok > least) & (base <= own)
            full = (base >= largest) & (base < own)
            pl.when(needed & full)(functools.partial(block, kv, j * tok, base, False))
            pl.when(needed & jnp.logical_not(full))(
                functools.partial(block, kv, j * tok, base, True)
            )
    if final:
        for h in range(heads):
            part = slice(h * tok, (h + 1) * tok)
            out[:, h * head : (h + 1) * head] = (acc[part, :head] / acc[part, head:]).astype(BF)
    else:
        out[...] = acc[...]


def attend(scal, q, start, index, kvs, at, acc=None, final=False):
    rows, head = q.shape
    tok = start.shape[0]
    layout = tuple(kv.shape[0] // tok for kv in kvs)
    first = acc is None
    args = [q, start, index, *kvs] + ([] if first else [acc])
    if final:
        shape = jax.ShapeDtypeStruct((tok, rows // tok * head), BF)
    else:
        shape = jax.ShapeDtypeStruct((rows, 2 * head), F32)
    blocks = sum(layout)
    return pl.pallas_call(
        functools.partial(attend_kernel, layout, at, first, final),
        in_specs=[pl.BlockSpec(memory_space=pltpu.SMEM)]
        + [pl.BlockSpec(memory_space=VMEM)] * len(args),
        out_specs=pl.BlockSpec(memory_space=VMEM),
        out_shape=shape,
        scratch_shapes=[pltpu.VMEM((rows, 2 * head), F32)],
        compiler_params=params(),
        cost_estimate=pl.CostEstimate(
            flops=blocks * rows * tok * head * 4,
            bytes_accessed=rows * head * 16,
            transcendentals=blocks * rows * tok,
        ),
        name="attend",
    )(scal, *args)


def out_kernel(targets, a_ref, b_ref, wa, wb, *outs):
    for n, (target, out) in enumerate(zip(targets, outs)):
        s = jnp.dot(a_ref[...], wa[target], preferred_element_type=F32)
        s += jnp.dot(b_ref[...], wb[target], preferred_element_type=F32)
        out[...] = s.astype(out.dtype)


def out_project(targets, kinds, a, b, w_own, w_sib):
    rows, depth = a.shape
    cols = w_own.shape[2]
    vm = pl.BlockSpec(memory_space=VMEM)
    return pl.pallas_call(
        functools.partial(out_kernel, targets),
        in_specs=[vm] * 4,
        out_specs=[vm] * len(targets),
        out_shape=[jax.ShapeDtypeStruct((rows, cols), kind) for kind in kinds],
        compiler_params=params(),
        cost_estimate=pl.CostEstimate(
            flops=4 * rows * depth * cols * len(targets),
            bytes_accessed=4 * depth * cols * len(targets),
            transcendentals=0,
        ),
        name="out_project",
    )(a, b, w_own, w_sib)


def sum_kernel(mine, a, b, c, out):
    out[...] = (mine[...] + a[...].astype(F32) + b[...].astype(F32) + c[...].astype(F32)).astype(
        out.dtype
    )


def add_up(mine, others):
    vm = pl.BlockSpec(memory_space=VMEM)
    return pl.pallas_call(
        sum_kernel,
        in_specs=[vm] * 4,
        out_specs=vm,
        out_shape=jax.ShapeDtypeStruct(mine.shape, BF),
        compiler_params=params(),
        name="add_up",
    )(mine, *others)


def on_device(tokens, w_query, w_key, w_value, q_gain, k_gain, doc_lengths, w_out):
    tok, part = tokens.shape
    head = q_gain.shape[0]
    seqs, tps = lax.axis_size("seq"), lax.axis_size("tp")
    ny = 4
    nz = seqs // ny
    nx = tps // 2
    my_seq = lax.axis_index("seq")
    my_tp = lax.axis_index("tp")
    zi, yi = my_seq // ny, my_seq % ny
    xi, ci = my_tp // 2, my_tp % 2
    turn = 1 - 2 * ci

    def sibling(a):
        return lax.ppermute(a, "tp", [(i, i ^ 1) for i in range(tps)])

    def along_x(a, d):
        return lax.ppermute(
            a,
            "tp",
            [(i, (i // 2 + (d if i % 2 == 0 else -d)) % nx * 2 + i % 2) for i in range(tps)],
        )

    def along_y(a, d):
        return lax.ppermute(a, "seq", [(i, i // ny * ny + (i + d) % ny) for i in range(seqs)])

    def along_z(a, d):
        return lax.ppermute(a, "seq", [(i, (i // ny + d) % nz * ny + i % ny) for i in range(seqs)])

    def swap_y(a, turned):
        pairs = []
        for s in range(seqs):
            for t in range(tps):
                y = s % ny
                other = y ^ 1 if t % 2 == turned else ny - 1 - y
                pairs.append((s * tps + t, (s // ny * ny + other) * tps + t))
        return lax.ppermute(a, ("seq", "tp"), pairs)

    low, high = (xi - turn) % nx, (xi + turn) % nx
    far = (xi + 2) % nx
    sc = 1 - ci
    order = jnp.stack(
        [2 * xi + ci, 2 * xi + sc, 2 * low + ci, 2 * high + ci]
        + [2 * high + sc, 2 * low + sc, 2 * far + ci, 2 * far + sc]
        + [2 * far + ci, 2 * high + ci, 2 * low + ci, 2 * xi + ci]
        + [2 * far + sc, 2 * low + sc, 2 * high + sc, 2 * xi + sc]
    ).astype(jnp.int32)
    nq, nk = w_query.shape[1], w_key.shape[1]
    plan = []
    for k in range(tps):
        plan += [(0, 0, part, k, 0, k, 0, nq), (1, 0, part, k, 0, k, nq, nk)]
        plan += [(2, 0, part, k, 0, k, nq + nk, nk)]
    (w_in,) = stage(
        order, [w_query, w_key, w_value], tuple(plan), [(tps, part, nq + 2 * nk)], "stage_in"
    )
    cols = w_out.shape[1] // tps
    plan = [(0, 1, cols, tps + k, 0, k, 0, cols) for k in range(nx)]
    plan += [(0, 1, cols, tps + nx + k, 1, k, 0, cols) for k in range(nx)]
    w_own, w_send = stage(
        order, [w_out], tuple(plan), [(nx, w_out.shape[0], cols)] * 2, "stage_out"
    )

    token_index = my_seq * tok + jnp.arange(tok, dtype=jnp.int32)
    start = doc_tables(doc_lengths, token_index)
    cos, sin = rope_tables(token_index - start, head)
    y1 = jnp.where(ci == 0, yi ^ 1, ny - 1 - yi)
    y2 = jnp.where(ci == 0, ny - 1 - yi, yi ^ 1)
    y3 = jnp.where(ci == 0, y2 ^ 1, ny - 1 - y2)

    def base(k, y):
        return ((zi - k) * ny + y) * tok

    def mixed(y):
        return base(jnp.where(yi > y, 0, 4), y)

    groups = [
        [base(0, yi), base(1, yi), base(0, y1), base(1, y1)],
        [base(2, yi), base(4, yi), base(2, y1), base(4, y1), base(1, y2), base(1, y3)]
        + [mixed(y2), mixed(y3), base(3, yi), base(3, y1)],
        [base(2, y2), base(2, y3), base(3, y2), base(3, y3)],
    ]
    scal = jnp.stack([my_seq * tok, start[0], start[-1]] + sum(groups, [])).astype(jnp.int32)
    start_col, index_col = start[:, None], token_index[:, None]

    own = tokens
    a1, a3, a2 = along_x(own, 1), along_x(own, nx - 1), along_x(own, 2)
    b0 = sibling(own)
    acc = project([own, b0], w_in, 0)
    a1, w_in, scal = lax.optimization_barrier((a1, w_in, scal))
    b1 = sibling(a1)
    a3, acc = lax.optimization_barrier((a3, acc))
    b3 = sibling(a3)
    a2, cos, sin, w_own, w_send = lax.optimization_barrier((a2, cos, sin, w_own, w_send))
    b2 = sibling(a2)
    acc = project([a1, a3, b1, b3], w_in, 2, acc)
    queries, kv = project(
        [a2, b2], w_in, 6, acc, last=(cos, sin, q_gain[None, :], k_gain[None, :])
    )
    w_send, kv = lax.optimization_barrier((w_send, kv))
    w_sib = sibling(w_send)

    r0 = kv
    r1 = along_z(r0, 1)
    r4 = along_z(r0, 4)
    r2 = along_z(r1, 1)
    r3 = along_z(r2, 1)
    s01 = swap_y(jnp.concatenate([r0, r1], axis=0), 0)
    s24 = swap_y(jnp.concatenate([r2, r4], axis=0), 0)
    s0, s1, s2, s4 = s01[:tok], s01[tok:], s24[:tok], s24[tok:]
    near = swap_y(
        jnp.concatenate([r1, s1, jnp.where(y2 > yi, r0, r4), jnp.where(y2 > y1, s0, s4)], axis=0), 1
    )
    s3 = swap_y(r3, 0)
    last = swap_y(jnp.concatenate([r2, s2, r3, s3], axis=0), 1)

    attn = (scal, queries, start_col, index_col)
    o = attend(*attn, [r0, r1, s01], 0)
    o = attend(*attn, [r2, r4, s24, near, r3, s3], 4, o)
    attended = attend(*attn, [last], 14, o, final=True)

    attended_sib = sibling(attended)
    (p2,) = out_project((0,), (BF,), attended, attended_sib, w_own, w_sib)
    t2 = along_x(p2, 2)
    p1, p3 = out_project((1, 2), (BF, BF), attended, attended_sib, w_own, w_sib)
    t1 = along_x(p1, 1)
    t3 = along_x(p3, nx - 1)
    (mine,) = out_project((3,), (F32,), attended, attended_sib, w_own, w_sib)
    return add_up(mine, [t1, t2, t3])


def solution(mesh):
    return jax.shard_map(
        on_device,
        mesh=mesh,
        in_specs=(
            P("seq", "tp"),
            P(None, "tp"),
            P(None, "tp"),
            P(None, "tp"),
            P(),
            P(),
            P(),
            P("tp", None),
        ),
        out_specs=P("seq", "tp"),
        check_vma=False,
    )
```

```python
import functools
import math

import jax
import jax.numpy as jnp
from jax import lax
from jax.experimental import pallas as pl
from jax.experimental.pallas import tpu as pltpu
from jax.sharding import PartitionSpec as P

EPSILON = 1e-06
ROPE_THETA = 1000000.0
BF = jnp.bfloat16
F32 = jnp.float32
VMEM = pltpu.VMEM
VLIMIT = 24 * 1024 * 1024


def params():
    return pltpu.CompilerParams(vmem_limit_bytes=VLIMIT)


def doc_tables(doc_lengths, token_index):
    doc_ends = jnp.cumsum(doc_lengths)
    passed = (token_index[:, None] >= doc_ends[None, :]).astype(jnp.int32)
    return jnp.sum(passed * doc_lengths[None, :], axis=1)


def rope_tables(position, head_width):
    half = head_width // 2
    frequency = ROPE_THETA ** (-(jnp.arange(half, dtype=F32) * 2.0 / head_width))
    angles = position.astype(F32)[:, None] * frequency[None, :]
    cos, sin = jnp.cos(angles), jnp.sin(angles)
    return jnp.concatenate([cos, cos], axis=1), jnp.concatenate([-sin, sin], axis=1)


NX, NY = 4, 4


class Place:
    def __init__(self):
        seq, tp = lax.axis_index("seq"), lax.axis_index("tp")
        self.seq, self.z, self.y = seq, seq // NY, lax.rem(seq, NY)
        self.x, self.c = tp // 2, lax.rem(tp, 2)

        def flip(a):
            return a + 1 - 2 * lax.rem(a, 2)

        even = self.c == 0
        self.y1 = jnp.where(even, flip(self.y), NY - 1 - self.y)
        self.y2 = jnp.where(even, NY - 1 - self.y, flip(self.y))
        self.y3 = jnp.where(even, flip(self.y2), NY - 1 - self.y2)

    def chip(self, turn):
        return lax.rem(self.x + NX + turn * (1 - 2 * self.c), NX)

    def part(self, turn, other):
        return 2 * self.chip(turn) + (1 - self.c if other else self.c)

    def base(self, block, tok):
        back, who = block
        y = (self.y, self.y1, self.y2, self.y3)[who]
        if back is None:
            back = jnp.where(self.y > y, 0, 4)
        return ((self.z - back) * NY + y) * tok


def stage_kernel(plan, sources, *refs):
    ins, rest = refs[:sources], refs[sources:]
    outs, flag, sem = rest[:-2], rest[-2], rest[-1]
    place = Place()
    copies = []
    for n, (src, axis, size, (turn, other), dst, row, col, cols) in enumerate(plan):
        cut = pl.ds(pl.multiple_of(place.part(turn, other) * size, size), size)
        view = ins[src].at[cut, :] if axis == 0 else ins[src].at[:, cut]
        copies.append(
            pltpu.make_async_copy(view, outs[dst].at[row, :, col : col + cols], sem.at[n])
        )
    for c in copies:
        c.start()
    flag[...] = jnp.zeros_like(flag)
    for c in copies:
        c.wait()


FLAG = (8, 128)


def stage(arrays, plan, shapes, name):
    vm = pl.BlockSpec(memory_space=VMEM)
    return pl.pallas_call(
        functools.partial(stage_kernel, plan, len(arrays)),
        in_specs=[pl.BlockSpec(memory_space=pltpu.HBM)] * len(arrays),
        out_specs=[vm] * (len(shapes) + 1),
        out_shape=[VMEM(shape, BF) for shape in shapes] + [jax.ShapeDtypeStruct(FLAG, F32)],
        scratch_shapes=[pltpu.SemaphoreType.DMA((len(plan),))],
        compiler_params=params(),
        cost_estimate=pl.CostEstimate(
            flops=0, bytes_accessed=sum(4 * math.prod(shape) for shape in shapes), transcendentals=0
        ),
        name=name,
    )(*[pltpu.with_memory_space_constraint(a, pltpu.HBM) for a in arrays])


def after(flags, *arrays):
    out = lax.optimization_barrier((*arrays, *flags))
    return (*out[: len(arrays)], list(out[len(arrays) :]))


def pack_kernel(pieces, tok, count, *refs):
    ins, out, flag = refs[:count], refs[-2], refs[-1]
    flag[...] = jnp.zeros_like(flag)
    place = Place()
    here = (place.y, place.y1)
    for n, piece in enumerate(pieces):
        to = slice(n * tok, (n + 1) * tok)
        if len(piece) == 2:
            src, at = piece
            out[to, :] = ins[src][at * tok : (at + 1) * tok, :]
        else:
            who, one, two = piece
            later = place.y2 > here[who]

            def put(src, at, to=to):
                out[to, :] = ins[src][at * tok : (at + 1) * tok, :]

            pl.when(later)(functools.partial(put, *one))
            pl.when(jnp.logical_not(later))(functools.partial(put, *two))


def pack(arrays, pieces, tok, flags=()):
    vm = pl.BlockSpec(memory_space=VMEM)
    count = len(arrays)
    return pl.pallas_call(
        functools.partial(pack_kernel, tuple(pieces), tok, count),
        in_specs=[vm] * count + [pl.BlockSpec(memory_space=pl.ANY)] * len(flags),
        out_specs=[vm, vm],
        out_shape=[
            VMEM((len(pieces) * tok, arrays[0].shape[1]), BF),
            jax.ShapeDtypeStruct(FLAG, F32),
        ],
        compiler_params=params(),
        name="pack",
    )(*arrays, *flags)


def project_kernel(count, at, head, first, last, flags, *refs):
    chunks, w = refs[:count], refs[count]
    rest = refs[count + 1 :]
    outs = 2 if last else 1
    rest = rest[: len(rest) - flags - outs] + rest[len(rest) - outs :]
    total = None
    for k in range(count):
        prod = jnp.dot(chunks[k][...], w[at + k], preferred_element_type=F32)
        total = prod if total is None else total + prod
    if not first:
        total = total + rest[0][...]
        rest = rest[1:]
    if not last:
        rest[0][...] = total
        return
    cos_ref, sin_ref, qg, kg, q_out, kv_out = rest
    cos = cos_ref[...]
    sin = sin_ref[...]
    rows = total.shape[0]
    heads = total.shape[1] // head - 2

    def norm_rotate(x, gain):
        inv = lax.rsqrt(jnp.mean(x * x, axis=-1, keepdims=True) + EPSILON)
        x = x * inv * gain
        return (x * cos + pltpu.roll(x, head // 2, 1) * sin).astype(BF)

    kcol = heads * head
    kv_out[:, :head] = norm_rotate(total[:, kcol : kcol + head], kg[...])
    kv_out[:, head:] = total[:, kcol + head : kcol + 2 * head].astype(BF)
    for h in range(heads):
        q_out[h * rows : (h + 1) * rows, :] = norm_rotate(
            total[:, h * head : (h + 1) * head], qg[...]
        )


def project(chunks, w, at, acc=None, last=None, flags=()):
    count = len(chunks)
    rows, depth = chunks[0].shape
    width = w.shape[2]
    args = [*chunks, w] + ([] if acc is None else [acc]) + (list(last) if last else [])
    head = last[0].shape[1] if last else 128
    if last:
        heads = width // head - 2
        shape = [
            VMEM((heads * rows, head), BF),
            VMEM((rows, 2 * head), BF),
        ]
    else:
        shape = VMEM((rows, width), F32)
    vm = pl.BlockSpec(memory_space=VMEM)
    return pl.pallas_call(
        functools.partial(
            project_kernel, count, at, head, acc is None, last is not None, len(flags)
        ),
        in_specs=[vm] * len(args) + [pl.BlockSpec(memory_space=pl.ANY)] * len(flags),
        out_specs=[vm, vm] if last else vm,
        out_shape=shape,
        compiler_params=params(),
        cost_estimate=pl.CostEstimate(
            flops=4 * rows * depth * count * width,
            bytes_accessed=2 * depth * count * width,
            transcendentals=0,
        ),
        name="project",
    )(*args, *flags)


def attend_kernel(layout, first, final, flags, start_s, *refs):
    n = len(layout)
    q_ref, start_ref, index_ref = refs[:3]
    kvs = refs[3 : 3 + n]
    rest = refs[3 + n :]
    if first:
        out, flag, acc = rest[flags:]
    else:
        acc_in = rest[0]
        out, flag, acc = rest[1 + flags :]
    flag[...] = jnp.zeros_like(flag)
    rows, head = q_ref.shape
    tok = start_ref.shape[0]
    heads = rows // tok
    scale = math.log2(math.e) / math.sqrt(head)
    acc[...] = jnp.zeros_like(acc) if first else acc_in[...]
    place = Place()
    own = place.seq * tok
    least = start_s[0]
    ones = jnp.ones((tok, head), BF)

    def unit(kv, bases):
        for j, base in enumerate(bases):
            at = slice(j * tok, (j + 1) * tok)
            keys = kv[at, :head]
            values = jnp.concatenate([kv[at, head:], ones], axis=1)
            col = base + lax.broadcasted_iota(jnp.int32, (tok, tok), 1)
            keep = (col >= start_ref[...]) & (col <= index_ref[...])
            for h in range(heads):
                part = slice(h * tok, (h + 1) * tok)
                s = lax.dot_general(
                    q_ref[part, :], keys, (((1,), (1,)), ((), ())), preferred_element_type=F32
                )
                p = jnp.where(keep, jnp.exp2(s * scale), 0.0).astype(BF)
                acc[part, :] += jnp.dot(p, values, preferred_element_type=F32)

    for kv, blocks in zip(kvs, layout):
        bases = [place.base(block, tok) for block in blocks]
        if blocks[0] == (0, 0):
            unit(kv, bases)
            continue
        needed = functools.reduce(
            jnp.logical_or, [(base + tok > least) & (base <= own) for base in bases]
        )
        pl.when(needed)(functools.partial(unit, kv, bases))
    if final:
        for h in range(heads):
            part = slice(h * tok, (h + 1) * tok)
            out[:, h * head : (h + 1) * head] = (acc[part, :head] / acc[part, head:]).astype(BF)
    else:
        out[...] = acc[...]


def attend(start, queries, start_col, index_col, pieces, acc=None, final=False, flags=()):
    rows, head = queries.shape
    tok = start_col.shape[0]
    kvs = [kv for kv, _ in pieces]
    layout = tuple(tuple(blocks) for _, blocks in pieces)
    first = acc is None
    args = [queries, start_col, index_col, *kvs] + ([] if first else [acc])
    if final:
        shape = VMEM((tok, rows // tok * head), BF)
    else:
        shape = VMEM((rows, 2 * head), F32)
    blocks = sum(len(blocks) for blocks in layout)
    vm = pl.BlockSpec(memory_space=VMEM)
    return pl.pallas_call(
        functools.partial(attend_kernel, layout, first, final, len(flags)),
        in_specs=[pl.BlockSpec(memory_space=pltpu.SMEM)]
        + [vm] * len(args)
        + [pl.BlockSpec(memory_space=pl.ANY)] * len(flags),
        out_specs=[vm, vm],
        out_shape=[shape, jax.ShapeDtypeStruct(FLAG, F32)],
        scratch_shapes=[pltpu.VMEM((rows, 2 * head), F32)],
        compiler_params=params(),
        cost_estimate=pl.CostEstimate(
            flops=blocks * rows * tok * head * 8,
            bytes_accessed=rows * head * 16,
            transcendentals=blocks * rows * tok,
        ),
        name="attend",
    )(start, *args, *flags)


def out_kernel(targets, a_ref, b_ref, wa, wb, *outs):
    for n, (target, out) in enumerate(zip(targets, outs)):
        s = jnp.dot(a_ref[...], wa[target], preferred_element_type=F32)
        s += jnp.dot(b_ref[...], wb[target], preferred_element_type=F32)
        out[...] = s.astype(out.dtype)


def out_project(targets, kinds, a, b, w_own, w_sib):
    rows, depth = a.shape
    cols = w_own.shape[2]
    vm = pl.BlockSpec(memory_space=VMEM)
    return pl.pallas_call(
        functools.partial(out_kernel, targets),
        in_specs=[vm] * 4,
        out_specs=[vm] * len(targets),
        out_shape=[VMEM((rows, cols), kind) for kind in kinds],
        compiler_params=params(),
        cost_estimate=pl.CostEstimate(
            flops=4 * rows * depth * cols * len(targets),
            bytes_accessed=4 * depth * cols * len(targets),
            transcendentals=0,
        ),
        name="out_project",
    )(a, b, w_own, pltpu.with_memory_space_constraint(w_sib, VMEM))


def sum_kernel(mine, a, b, c, out):
    out[...] = (mine[...] + a[...].astype(F32) + b[...].astype(F32) + c[...].astype(F32)).astype(
        out.dtype
    )


def add_up(mine, others):
    vm = pl.BlockSpec(memory_space=VMEM)
    return pl.pallas_call(
        sum_kernel,
        in_specs=[vm] * 4,
        out_specs=vm,
        out_shape=jax.ShapeDtypeStruct(mine.shape, BF),
        compiler_params=params(),
        name="add_up",
    )(mine, *others)


def on_device(tokens, w_query, w_key, w_value, q_gain, k_gain, doc_lengths, w_out):
    tok, part = tokens.shape
    head = q_gain.shape[0]
    seqs, tps = lax.axis_size("seq"), lax.axis_size("tp")
    ny = 4
    nz = seqs // ny
    nx = tps // 2
    my_seq = lax.axis_index("seq")

    def sibling(a):
        return lax.ppermute(a, "tp", [(i, i ^ 1) for i in range(tps)])

    def along_x(a, d):
        return lax.ppermute(
            a,
            "tp",
            [(i, (i // 2 + (d if i % 2 == 0 else -d)) % nx * 2 + i % 2) for i in range(tps)],
        )

    def along_y(a, d):
        return lax.ppermute(a, "seq", [(i, i // ny * ny + (i + d) % ny) for i in range(seqs)])

    def along_z(a, d):
        return lax.ppermute(a, "seq", [(i, (i // ny + d) % nz * ny + i % ny) for i in range(seqs)])

    def swap_y(a, turned):
        pairs = []
        for s in range(seqs):
            for t in range(tps):
                y = s % ny
                other = y ^ 1 if t % 2 == turned else ny - 1 - y
                pairs.append((s * tps + t, (s // ny * ny + other) * tps + t))
        return lax.ppermute(a, ("seq", "tp"), pairs)

    nq, nk = w_query.shape[1], w_key.shape[1]
    arrivals = [(0, 0), (0, 1), (-1, 0), (1, 0), (1, 1), (-1, 1), (2, 0), (2, 1)]
    plan = []
    for k, shard in enumerate(arrivals):
        plan += [(0, 0, part, shard, 0, k, 0, nq), (1, 0, part, shard, 0, k, nq, nk)]
        plan += [(2, 0, part, shard, 0, k, nq + nk, nk)]
    w_in, flag_in = stage(
        [w_query, w_key, w_value], tuple(plan), [(tps, part, nq + 2 * nk)], "stage_in"
    )
    cols = w_out.shape[1] // tps
    plan = [(0, 1, cols, (d, 0), 0, k, 0, cols) for k, d in enumerate((2, 1, -1, 0))]
    plan += [(0, 1, cols, (d, 1), 1, k, 0, cols) for k, d in enumerate((2, -1, 1, 0))]
    w_own, w_send, flag_out = stage(
        [w_out], tuple(plan), [(nx, w_out.shape[0], cols)] * 2, "stage_out"
    )

    token_index = my_seq * tok + jnp.arange(tok, dtype=jnp.int32)
    start = doc_tables(doc_lengths, token_index)
    cos, sin = rope_tables(token_index - start, head)
    start_col, index_col = start[:, None], token_index[:, None]

    own = tokens
    a1, a3, a2 = along_x(own, 1), along_x(own, nx - 1), along_x(own, 2)
    b0 = sibling(own)
    acc = project([own, b0], w_in, 0)
    a1, flags = after([flag_in], a1)
    b1 = sibling(a1)
    a3, acc, _ = after([], a3, acc)
    b3 = sibling(a3)
    a2, cos, sin, start_col, index_col, more = after(
        [flag_out], a2, cos, sin, start_col, index_col
    )
    b2 = sibling(a2)
    acc = project([a1, a3, b1, b3], w_in, 2, acc, flags=flags)
    queries, kv = project(
        [a2, b2], w_in, 6, acc, last=(cos, sin, q_gain[None, :], k_gain[None, :]), flags=more
    )
    w_send, kv = lax.optimization_barrier((w_send, kv))
    w_sib = sibling(w_send)

    attn = (start, queries, start_col, index_col)
    r0 = kv
    r1 = along_z(r0, 1)
    r4 = along_z(r0, 4)
    r2 = along_z(r1, 1)
    r3 = along_z(r1, 2)
    x01, _ = pack([r0, r1], [(0, 0), (1, 0)], tok)
    s01 = swap_y(x01, 0)
    o, flag_a = attend(*attn, [(r0, [(0, 0)]), (r1, [(1, 0)])])
    x_near, flag_n = pack([r1, s01], [(0, 0), (1, 1)], tok)
    near = swap_y(x_near, 1)
    x234, _ = pack([r2, r3, r4], [(0, 0), (1, 0), (2, 0)], tok, flags=[flag_a, flag_n])
    s234 = swap_y(x234, 0)
    o, flag_b = attend(
        *attn,
        [(s01, [(0, 1), (1, 1)]), (r2, [(2, 0)]), (r3, [(3, 0)]), (r4, [(4, 0)])],
        o,
    )
    x_last, flag_l = pack(
        [r2, r3, s234, r0, r4, s01],
        [(0, 0), (1, 0), (2, 0), (2, 1), (0, (3, 0), (4, 0)), (1, (5, 0), (2, 2))],
        tok,
        flags=[flag_b, near],
    )
    last = swap_y(x_last, 1)
    o, _ = attend(
        *attn,
        [(near, [(1, 2), (1, 3)]), (s234, [(2, 1), (3, 1), (4, 1)])],
        o,
        flags=[flag_l],
    )
    attended, _ = attend(
        *attn,
        [(last, [(2, 2), (3, 2), (2, 3), (3, 3), (None, 2), (None, 3)])],
        o,
        final=True,
    )

    attended_sib = sibling(attended)
    (p2,) = out_project((0,), (BF,), attended, attended_sib, w_own, w_sib)
    t2 = along_x(p2, 2)
    p1, p3 = out_project((1, 2), (BF, BF), attended, attended_sib, w_own, w_sib)
    t1 = along_x(p1, 1)
    t3 = along_x(p3, nx - 1)
    (mine,) = out_project((3,), (F32,), attended, attended_sib, w_own, w_sib)
    return add_up(mine, [t1, t2, t3])


def solution(mesh):
    return jax.shard_map(
        on_device,
        mesh=mesh,
        in_specs=(
            P("seq", "tp"),
            P(None, "tp"),
            P(None, "tp"),
            P(None, "tp"),
            P(),
            P(),
            P(),
            P("tp", None),
        ),
        out_specs=P("seq", "tp"),
        check_vma=False,
    )
```

```python
import functools
import math

import jax
import jax.numpy as jnp
from jax import lax
from jax.experimental import pallas as pl
from jax.experimental.pallas import tpu as pltpu
from jax.sharding import PartitionSpec as P

EPSILON = 1e-06
ROPE_THETA = 1000000.0
BF = jnp.bfloat16
F32 = jnp.float32
VMEM = pltpu.VMEM
MIB = 1024 * 1024


def params(limit=10):
    return pltpu.CompilerParams(vmem_limit_bytes=limit * MIB)


def doc_tables(doc_lengths, token_index):
    doc_ends = jnp.cumsum(doc_lengths)
    passed = (token_index[:, None] >= doc_ends[None, :]).astype(jnp.int32)
    return jnp.sum(passed * doc_lengths[None, :], axis=1)


def rope_tables(position, head_width):
    half = head_width // 2
    frequency = ROPE_THETA ** (-(jnp.arange(half, dtype=F32) * 2.0 / head_width))
    angles = position.astype(F32)[:, None] * frequency[None, :]
    cos, sin = jnp.cos(angles), jnp.sin(angles)
    return jnp.concatenate([cos, cos], axis=1), jnp.concatenate([-sin, sin], axis=1)


NX, NY = 4, 4


class Place:
    def __init__(self):
        seq, tp = lax.axis_index("seq"), lax.axis_index("tp")
        self.seq, self.z, self.y = seq, seq // NY, lax.rem(seq, NY)
        self.x, self.c = tp // 2, lax.rem(tp, 2)

        def flip(a):
            return a + 1 - 2 * lax.rem(a, 2)

        even = self.c == 0
        self.y1 = jnp.where(even, flip(self.y), NY - 1 - self.y)
        self.y2 = jnp.where(even, NY - 1 - self.y, flip(self.y))
        self.y3 = jnp.where(even, flip(self.y2), NY - 1 - self.y2)

    def chip(self, turn):
        return lax.rem(self.x + NX + turn * (1 - 2 * self.c), NX)

    def part(self, turn, other):
        return 2 * self.chip(turn) + (1 - self.c if other else self.c)

    def base(self, block, tok):
        back, who = block
        y = (self.y, self.y1, self.y2, self.y3)[who]
        if back is None:
            back = jnp.where(self.y > y, 0, 4)
        return ((self.z - back) * NY + y) * tok


def stage_kernel(plan, sources, *refs):
    ins, rest = refs[:sources], refs[sources:]
    outs, flag, sem = rest[:-2], rest[-2], rest[-1]
    place = Place()
    copies = []
    for n, (src, axis, size, (turn, other), dst, row, col, cols) in enumerate(plan):
        cut = pl.ds(pl.multiple_of(place.part(turn, other) * size, size), size)
        view = ins[src].at[cut, :] if axis == 0 else ins[src].at[:, cut]
        copies.append(
            pltpu.make_async_copy(view, outs[dst].at[row, :, col : col + cols], sem.at[n])
        )
    for c in copies:
        c.start()
    flag[...] = jnp.zeros_like(flag)
    for c in copies:
        c.wait()


FLAG = (8, 128)


def fetch_kernel(src, out, flag, sem):
    copy = pltpu.make_async_copy(src, out, sem)
    copy.start()
    flag[...] = jnp.zeros_like(flag)
    copy.wait()


def fetch(a):
    vm = pl.BlockSpec(memory_space=VMEM)
    return pl.pallas_call(
        fetch_kernel,
        in_specs=[pl.BlockSpec(memory_space=pl.ANY)],
        out_specs=[vm, vm],
        out_shape=[VMEM(a.shape, a.dtype), jax.ShapeDtypeStruct(FLAG, F32)],
        scratch_shapes=[pltpu.SemaphoreType.DMA],
        compiler_params=params(),
        name="fetch",
    )(a)


def stage(arrays, plan, shapes, name):
    vm = pl.BlockSpec(memory_space=VMEM)
    return pl.pallas_call(
        functools.partial(stage_kernel, plan, len(arrays)),
        in_specs=[pl.BlockSpec(memory_space=pltpu.HBM)] * len(arrays),
        out_specs=[vm] * (len(shapes) + 1),
        out_shape=[VMEM(shape, BF) for shape in shapes] + [jax.ShapeDtypeStruct(FLAG, F32)],
        scratch_shapes=[pltpu.SemaphoreType.DMA((len(plan),))],
        compiler_params=params(14),
        cost_estimate=pl.CostEstimate(
            flops=0, bytes_accessed=sum(4 * math.prod(shape) for shape in shapes), transcendentals=0
        ),
        name=name,
    )(*[pltpu.with_memory_space_constraint(a, pltpu.HBM) for a in arrays])


def after(flags, *arrays):
    out = lax.optimization_barrier((*arrays, *flags))
    return (*out[: len(arrays)], list(out[len(arrays) :]))


def hold_kernel(*refs):
    refs[-1][...] = jnp.zeros(FLAG, F32)


def hold(*arrays):
    return pl.pallas_call(
        hold_kernel,
        in_specs=[pl.BlockSpec(memory_space=pl.ANY)] * len(arrays),
        out_specs=pl.BlockSpec(memory_space=VMEM),
        out_shape=jax.ShapeDtypeStruct(FLAG, F32),
        compiler_params=params(),
        cost_estimate=pl.CostEstimate(flops=2 * 10**10, bytes_accessed=4096, transcendentals=0),
        name="hold",
    )(*arrays)


def pack_kernel(pieces, tok, count, *refs):
    ins, out, flag = refs[:count], refs[-2], refs[-1]
    flag[...] = jnp.zeros_like(flag)
    place = Place()
    here = (place.y, place.y1)
    for n, piece in enumerate(pieces):
        to = slice(n * tok, (n + 1) * tok)
        if len(piece) == 2:
            src, at = piece
            out[to, :] = ins[src][at * tok : (at + 1) * tok, :]
        else:
            who, one, two = piece
            later = place.y2 > here[who]

            def put(src, at, to=to):
                out[to, :] = ins[src][at * tok : (at + 1) * tok, :]

            pl.when(later)(functools.partial(put, *one))
            pl.when(jnp.logical_not(later))(functools.partial(put, *two))


def pack(arrays, pieces, tok, flags=()):
    vm = pl.BlockSpec(memory_space=VMEM)
    count = len(arrays)
    return pl.pallas_call(
        functools.partial(pack_kernel, tuple(pieces), tok, count),
        in_specs=[vm] * count + [pl.BlockSpec(memory_space=pl.ANY)] * len(flags),
        out_specs=[vm, vm],
        out_shape=[
            VMEM((len(pieces) * tok, arrays[0].shape[1]), BF),
            jax.ShapeDtypeStruct(FLAG, F32),
        ],
        compiler_params=params(),
        name="pack",
    )(*arrays, *flags)


def project_kernel(count, at, head, first, last, flags, *refs):
    chunks, w = refs[:count], refs[count]
    rest = refs[count + 1 :]
    outs = 2 if last else 1
    rest = rest[: len(rest) - flags - outs] + rest[len(rest) - outs :]
    total = None
    for k in range(count):
        prod = jnp.dot(chunks[k][...], w[at + k], preferred_element_type=F32)
        total = prod if total is None else total + prod
    if not first:
        total = total + rest[0][...]
        rest = rest[1:]
    if not last:
        rest[0][...] = total
        return
    cos_ref, sin_ref, qg, kg, q_out, kv_out = rest
    cos = cos_ref[...]
    sin = sin_ref[...]
    rows = total.shape[0]
    heads = total.shape[1] // head - 2

    def norm_rotate(x, gain):
        inv = lax.rsqrt(jnp.mean(x * x, axis=-1, keepdims=True) + EPSILON)
        x = x * inv * gain
        return (x * cos + pltpu.roll(x, head // 2, 1) * sin).astype(BF)

    kcol = heads * head
    kv_out[:, :head] = norm_rotate(total[:, kcol : kcol + head], kg[...])
    kv_out[:, head:] = total[:, kcol + head : kcol + 2 * head].astype(BF)
    for h in range(heads):
        q_out[h * rows : (h + 1) * rows, :] = norm_rotate(
            total[:, h * head : (h + 1) * head], qg[...]
        )


def project(chunks, w, at, acc=None, last=None, flags=()):
    count = len(chunks)
    rows, depth = chunks[0].shape
    width = w.shape[2]
    args = [*chunks, w] + ([] if acc is None else [acc]) + (list(last) if last else [])
    head = last[0].shape[1] if last else 128
    if last:
        heads = width // head - 2
        shape = [
            VMEM((heads * rows, head), BF),
            VMEM((rows, 2 * head), BF),
        ]
    else:
        shape = VMEM((rows, width), F32)
    vm = pl.BlockSpec(memory_space=VMEM)
    return pl.pallas_call(
        functools.partial(
            project_kernel, count, at, head, acc is None, last is not None, len(flags)
        ),
        in_specs=[vm] * len(args) + [pl.BlockSpec(memory_space=pl.ANY)] * len(flags),
        out_specs=[vm, vm] if last else vm,
        out_shape=shape,
        compiler_params=params(16),
        cost_estimate=pl.CostEstimate(
            flops=4 * rows * depth * count * width,
            bytes_accessed=2 * depth * count * width,
            transcendentals=0,
        ),
        name="project",
    )(*args, *flags)


def attend_kernel(layout, first, final, flags, start_s, *refs):
    n = len(layout)
    q_ref, start_ref, index_ref = refs[:3]
    kvs = refs[3 : 3 + n]
    rest = refs[3 + n :]
    if first:
        out, flag, acc = rest[flags:]
    else:
        acc_in = rest[0]
        out, flag, acc = rest[1 + flags :]
    flag[...] = jnp.zeros_like(flag)
    rows, head = q_ref.shape
    tok = start_ref.shape[0]
    heads = rows // tok
    scale = math.log2(math.e) / math.sqrt(head)
    acc[...] = jnp.zeros_like(acc) if first else acc_in[...]
    place = Place()
    own = place.seq * tok
    least = start_s[0]
    ones = jnp.ones((tok, head), BF)

    def unit(kv, bases):
        for j, base in enumerate(bases):
            at = slice(j * tok, (j + 1) * tok)
            keys = kv[at, :head]
            values = jnp.concatenate([kv[at, head:], ones], axis=1)
            col = base + lax.broadcasted_iota(jnp.int32, (tok, tok), 1)
            keep = (col >= start_ref[...]) & (col <= index_ref[...])
            for h in range(heads):
                part = slice(h * tok, (h + 1) * tok)
                s = lax.dot_general(
                    q_ref[part, :], keys, (((1,), (1,)), ((), ())), preferred_element_type=F32
                )
                p = jnp.where(keep, jnp.exp2(s * scale), 0.0).astype(BF)
                acc[part, :] += jnp.dot(p, values, preferred_element_type=F32)

    for kv, blocks in zip(kvs, layout):
        bases = [place.base(block, tok) for block in blocks]
        if blocks[0] == (0, 0):
            unit(kv, bases)
            continue
        needed = functools.reduce(
            jnp.logical_or, [(base + tok > least) & (base <= own) for base in bases]
        )
        pl.when(needed)(functools.partial(unit, kv, bases))
    if final:
        for h in range(heads):
            part = slice(h * tok, (h + 1) * tok)
            out[:, h * head : (h + 1) * head] = (acc[part, :head] / acc[part, head:]).astype(BF)
    else:
        out[...] = acc[...]


def attend(start, queries, start_col, index_col, pieces, acc=None, final=False, flags=()):
    rows, head = queries.shape
    tok = start_col.shape[0]
    kvs = [kv for kv, _ in pieces]
    layout = tuple(tuple(blocks) for _, blocks in pieces)
    first = acc is None
    args = [queries, start_col, index_col, *kvs] + ([] if first else [acc])
    if final:
        shape = VMEM((tok, rows // tok * head), BF)
    else:
        shape = VMEM((rows, 2 * head), F32)
    blocks = sum(len(blocks) for blocks in layout)
    vm = pl.BlockSpec(memory_space=VMEM)
    return pl.pallas_call(
        functools.partial(attend_kernel, layout, first, final, len(flags)),
        in_specs=[pl.BlockSpec(memory_space=pltpu.SMEM)]
        + [vm] * len(args)
        + [pl.BlockSpec(memory_space=pl.ANY)] * len(flags),
        out_specs=[vm, vm],
        out_shape=[shape, jax.ShapeDtypeStruct(FLAG, F32)],
        scratch_shapes=[pltpu.VMEM((rows, 2 * head), F32)],
        compiler_params=params(),
        cost_estimate=pl.CostEstimate(
            flops=blocks * rows * tok * head * 8,
            bytes_accessed=rows * head * 16,
            transcendentals=blocks * rows * tok,
        ),
        name="attend",
    )(start, *args, *flags)


def out_kernel(targets, a_ref, b_ref, wa, wb, *outs):
    for n, (target, out) in enumerate(zip(targets, outs)):
        s = jnp.dot(a_ref[...], wa[target], preferred_element_type=F32)
        s += jnp.dot(b_ref[...], wb[target], preferred_element_type=F32)
        out[...] = s.astype(out.dtype)


def out_project(targets, kinds, a, b, w_own, w_sib):
    rows, depth = a.shape
    cols = w_own.shape[2]
    vm = pl.BlockSpec(memory_space=VMEM)
    return pl.pallas_call(
        functools.partial(out_kernel, targets),
        in_specs=[vm] * 4,
        out_specs=[vm] * len(targets),
        out_shape=[VMEM((rows, cols), kind) for kind in kinds],
        compiler_params=params(),
        cost_estimate=pl.CostEstimate(
            flops=4 * rows * depth * cols * len(targets),
            bytes_accessed=4 * depth * cols * len(targets),
            transcendentals=0,
        ),
        name="out_project",
    )(a, b, w_own, w_sib)


def sum_kernel(mine, a, b, c, out):
    out[...] = (mine[...] + a[...].astype(F32) + b[...].astype(F32) + c[...].astype(F32)).astype(
        out.dtype
    )


def add_up(mine, others):
    vm = pl.BlockSpec(memory_space=VMEM)
    return pl.pallas_call(
        sum_kernel,
        in_specs=[vm] * 4,
        out_specs=vm,
        out_shape=jax.ShapeDtypeStruct(mine.shape, BF),
        compiler_params=params(),
        name="add_up",
    )(mine, *others)


def on_device(tokens, w_query, w_key, w_value, q_gain, k_gain, doc_lengths, w_out):
    tok, part = tokens.shape
    head = q_gain.shape[0]
    seqs, tps = lax.axis_size("seq"), lax.axis_size("tp")
    ny = 4
    nz = seqs // ny
    nx = tps // 2
    my_seq = lax.axis_index("seq")

    def sibling(a):
        return lax.ppermute(a, "tp", [(i, i ^ 1) for i in range(tps)])

    def along_x(a, d):
        return lax.ppermute(
            a,
            "tp",
            [(i, (i // 2 + (d if i % 2 == 0 else -d)) % nx * 2 + i % 2) for i in range(tps)],
        )

    def along_y(a, d):
        return lax.ppermute(a, "seq", [(i, i // ny * ny + (i + d) % ny) for i in range(seqs)])

    def along_z(a, d):
        return lax.ppermute(a, "seq", [(i, (i // ny + d) % nz * ny + i % ny) for i in range(seqs)])

    def swap_y(a, turned):
        pairs = []
        for s in range(seqs):
            for t in range(tps):
                y = s % ny
                other = y ^ 1 if t % 2 == turned else ny - 1 - y
                pairs.append((s * tps + t, (s // ny * ny + other) * tps + t))
        return lax.ppermute(a, ("seq", "tp"), pairs)

    nq, nk = w_query.shape[1], w_key.shape[1]
    arrivals = [(0, 0), (0, 1), (-1, 0), (1, 0), (1, 1), (-1, 1), (2, 0), (2, 1)]
    plan = []
    for k, shard in enumerate(arrivals):
        plan += [(0, 0, part, shard, 0, k, 0, nq), (1, 0, part, shard, 0, k, nq, nk)]
        plan += [(2, 0, part, shard, 0, k, nq + nk, nk)]
    w_in, flag_in = stage(
        [w_query, w_key, w_value], tuple(plan), [(tps, part, nq + 2 * nk)], "stage_in"
    )
    cols = w_out.shape[1] // tps
    plan = [(0, 1, cols, (d, 0), 0, k, 0, cols) for k, d in enumerate((2, 1, -1, 0))]
    plan += [(0, 1, cols, (d, 1), 1, k, 0, cols) for k, d in enumerate((2, -1, 1, 0))]
    w_own, w_send, flag_out = stage(
        [w_out], tuple(plan), [(nx, w_out.shape[0], cols)] * 2, "stage_out"
    )

    token_index = my_seq * tok + jnp.arange(tok, dtype=jnp.int32)
    start = doc_tables(doc_lengths, token_index)
    cos, sin = rope_tables(token_index - start, head)
    start_col, index_col = start[:, None], token_index[:, None]

    own = tokens
    a1, a3, a2 = along_x(own, 1), along_x(own, nx - 1), along_x(own, 2)
    b0 = sibling(own)
    acc = project([own, b0], w_in, 0)
    a1, flags = after([flag_in, flag_out], a1)
    b1 = sibling(a1)
    a3, acc, _ = after([], a3, acc)
    b3 = sibling(a3)
    a2, cos, sin, start_col, index_col, _ = after([], a2, cos, sin, start_col, index_col)
    b2 = sibling(a2)
    acc = project([a1, a3, b1, b3], w_in, 2, acc, flags=flags)
    queries, kv = project(
        [a2, b2], w_in, 6, acc, last=(cos, sin, q_gain[None, :], k_gain[None, :])
    )
    attn = (start, queries, start_col, index_col)
    r0 = kv
    r1 = along_z(r0, 1)
    r4 = along_z(r0, 4)
    r2 = along_z(r1, 1)
    r3 = along_z(r2, 1)
    x012, _ = pack([r0, r1, r2], [(0, 0), (1, 0), (2, 0)], tok)
    s012 = swap_y(x012, 0)
    o, _ = attend(*attn, [(r0, [(0, 0)]), (r1, [(1, 0)])])
    x34, flag_34 = pack([r3, r4], [(0, 0), (1, 0)], tok)
    s34 = swap_y(x34, 0)
    x_near, flag_n = pack(
        [r1, r2, s012], [(0, 0), (1, 0), (2, 1), (2, 2)], tok, flags=[hold(r3, r4), flag_34]
    )
    near = swap_y(x_near, 1)
    w_send, flags = after([flag_n], w_send)
    w_sib = sibling(w_send)
    o, flag_b = attend(*attn, [(r2, [(2, 0)]), (s012, [(0, 1), (1, 1), (2, 1)])], o, flags=flags)
    x_last, flag_l = pack(
        [r3, s34, r0, r4, s012],
        [(0, 0), (1, 0), (0, (2, 0), (3, 0)), (1, (4, 0), (1, 1))],
        tok,
        flags=[flag_b, hold(s34), near],
    )
    last = swap_y(x_last, 1)
    w_sib, flag_w = fetch(w_sib)
    o, _ = attend(
        *attn,
        [
            (near, [(1, 2), (2, 2), (1, 3), (2, 3)]),
            (r3, [(3, 0)]),
            (r4, [(4, 0)]),
            (s34, [(3, 1), (4, 1)]),
        ],
        o,
        flags=[flag_l, flag_w],
    )
    attended, _ = attend(
        *attn, [(last, [(3, 2), (3, 3), (None, 2), (None, 3)])], o, final=True
    )

    attended_sib = sibling(attended)
    (p2,) = out_project((0,), (BF,), attended, attended_sib, w_own, w_sib)
    t2 = along_x(p2, 2)
    p1, p3 = out_project((1, 2), (BF, BF), attended, attended_sib, w_own, w_sib)
    t1 = along_x(p1, 1)
    t3 = along_x(p3, nx - 1)
    (mine,) = out_project((3,), (F32,), attended, attended_sib, w_own, w_sib)
    return add_up(mine, [t1, t2, t3])


def solution(mesh):
    return jax.shard_map(
        on_device,
        mesh=mesh,
        in_specs=(
            P("seq", "tp"),
            P(None, "tp"),
            P(None, "tp"),
            P(None, "tp"),
            P(),
            P(),
            P(),
            P("tp", None),
        ),
        out_specs=P("seq", "tp"),
        check_vma=False,
    )
```

```python
import functools
import math

import jax
import jax.numpy as jnp
from jax import lax
from jax.experimental import pallas as pl
from jax.experimental.pallas import tpu as pltpu
from jax.sharding import PartitionSpec as P

EPSILON = 1e-06
ROPE_THETA = 1000000.0
BF = jnp.bfloat16
F32 = jnp.float32
VMEM = pltpu.VMEM
MIB = 1024 * 1024


def params(limit=10):
    return pltpu.CompilerParams(vmem_limit_bytes=limit * MIB)


def doc_tables(doc_lengths, token_index):
    doc_ends = jnp.cumsum(doc_lengths)
    passed = (token_index[:, None] >= doc_ends[None, :]).astype(jnp.int32)
    return jnp.sum(passed * doc_lengths[None, :], axis=1)


def rope_tables(position, head_width):
    half = head_width // 2
    frequency = ROPE_THETA ** (-(jnp.arange(half, dtype=F32) * 2.0 / head_width))
    angles = position.astype(F32)[:, None] * frequency[None, :]
    cos, sin = jnp.cos(angles), jnp.sin(angles)
    return jnp.concatenate([cos, cos], axis=1), jnp.concatenate([-sin, sin], axis=1)


NX, NY = 4, 4


class Place:
    def __init__(self):
        seq, tp = lax.axis_index("seq"), lax.axis_index("tp")
        self.seq, self.z, self.y = seq, seq // NY, lax.rem(seq, NY)
        self.x, self.c = tp // 2, lax.rem(tp, 2)

        def flip(a):
            return a + 1 - 2 * lax.rem(a, 2)

        even = self.c == 0
        self.y1 = jnp.where(even, flip(self.y), NY - 1 - self.y)
        self.y2 = jnp.where(even, NY - 1 - self.y, flip(self.y))
        self.y3 = jnp.where(even, flip(self.y2), NY - 1 - self.y2)

    def chip(self, turn):
        return lax.rem(self.x + NX + turn * (1 - 2 * self.c), NX)

    def part(self, turn, other):
        return 2 * self.chip(turn) + (1 - self.c if other else self.c)

    def base(self, block, tok):
        back, who = block
        y = (self.y, self.y1, self.y2, self.y3)[who]
        if back is None:
            back = jnp.where(self.y > y, 0, 4)
        return ((self.z - back) * NY + y) * tok


def stage_kernel(plan, sources, *refs):
    ins, rest = refs[:sources], refs[sources:]
    outs, flag, sem = rest[:-2], rest[-2], rest[-1]
    place = Place()
    copies = []
    for n, (src, axis, size, (turn, other), dst, row, col, cols) in enumerate(plan):
        cut = pl.ds(pl.multiple_of(place.part(turn, other) * size, size), size)
        view = ins[src].at[cut, :] if axis == 0 else ins[src].at[:, cut]
        copies.append(
            pltpu.make_async_copy(view, outs[dst].at[row, :, col : col + cols], sem.at[n])
        )
    for c in copies:
        c.start()
    flag[...] = jnp.zeros_like(flag)
    for c in copies:
        c.wait()


FLAG = (8, 128)


def fetch_kernel(src, out, flag, sem):
    copy = pltpu.make_async_copy(src, out, sem)
    copy.start()
    flag[...] = jnp.zeros_like(flag)
    copy.wait()


def fetch(a):
    vm = pl.BlockSpec(memory_space=VMEM)
    return pl.pallas_call(
        fetch_kernel,
        in_specs=[pl.BlockSpec(memory_space=pl.ANY)],
        out_specs=[vm, vm],
        out_shape=[VMEM(a.shape, a.dtype), jax.ShapeDtypeStruct(FLAG, F32)],
        scratch_shapes=[pltpu.SemaphoreType.DMA],
        compiler_params=params(),
        name="fetch",
    )(a)


def stage(arrays, plan, shapes, name):
    vm = pl.BlockSpec(memory_space=VMEM)
    return pl.pallas_call(
        functools.partial(stage_kernel, plan, len(arrays)),
        in_specs=[pl.BlockSpec(memory_space=pltpu.HBM)] * len(arrays),
        out_specs=[vm] * (len(shapes) + 1),
        out_shape=[VMEM(shape, BF) for shape in shapes] + [jax.ShapeDtypeStruct(FLAG, F32)],
        scratch_shapes=[pltpu.SemaphoreType.DMA((len(plan),))],
        compiler_params=params(14),
        cost_estimate=pl.CostEstimate(
            flops=0, bytes_accessed=sum(4 * math.prod(shape) for shape in shapes), transcendentals=0
        ),
        name=name,
    )(*[pltpu.with_memory_space_constraint(a, pltpu.HBM) for a in arrays])


def after(flags, *arrays):
    out = lax.optimization_barrier((*arrays, *flags))
    return (*out[: len(arrays)], list(out[len(arrays) :]))


def hold_kernel(*refs):
    refs[-1][...] = jnp.zeros(FLAG, F32)


def hold(*arrays):
    return pl.pallas_call(
        hold_kernel,
        in_specs=[pl.BlockSpec(memory_space=pl.ANY)] * len(arrays),
        out_specs=pl.BlockSpec(memory_space=VMEM),
        out_shape=jax.ShapeDtypeStruct(FLAG, F32),
        compiler_params=params(),
        cost_estimate=pl.CostEstimate(flops=2 * 10**10, bytes_accessed=4096, transcendentals=0),
        name="hold",
    )(*arrays)


def pack_kernel(pieces, tok, count, *refs):
    ins, out, flag = refs[:count], refs[-2], refs[-1]
    flag[...] = jnp.zeros_like(flag)
    place = Place()
    here = (place.y, place.y1)
    for n, piece in enumerate(pieces):
        to = slice(n * tok, (n + 1) * tok)
        if len(piece) == 2:
            src, at = piece
            out[to, :] = ins[src][at * tok : (at + 1) * tok, :]
        else:
            who, one, two = piece
            later = place.y2 > here[who]

            def put(src, at, to=to):
                out[to, :] = ins[src][at * tok : (at + 1) * tok, :]

            pl.when(later)(functools.partial(put, *one))
            pl.when(jnp.logical_not(later))(functools.partial(put, *two))


def pack(arrays, pieces, tok, flags=()):
    vm = pl.BlockSpec(memory_space=VMEM)
    count = len(arrays)
    return pl.pallas_call(
        functools.partial(pack_kernel, tuple(pieces), tok, count),
        in_specs=[vm] * count + [pl.BlockSpec(memory_space=pl.ANY)] * len(flags),
        out_specs=[vm, vm],
        out_shape=[
            VMEM((len(pieces) * tok, arrays[0].shape[1]), BF),
            jax.ShapeDtypeStruct(FLAG, F32),
        ],
        compiler_params=params(),
        name="pack",
    )(*arrays, *flags)


def project_kernel(count, at, head, first, last, flags, *refs):
    chunks, w = refs[:count], refs[count]
    rest = refs[count + 1 :]
    outs = 2 if last else 1
    rest = rest[: len(rest) - flags - outs] + rest[len(rest) - outs :]
    total = None
    for k in range(count):
        prod = jnp.dot(chunks[k][...], w[at + k], preferred_element_type=F32)
        total = prod if total is None else total + prod
    if not first:
        total = total + rest[0][...]
        rest = rest[1:]
    if not last:
        rest[0][...] = total
        return
    cos_ref, sin_ref, qg, kg, q_out, kv_out = rest
    cos = cos_ref[...]
    sin = sin_ref[...]
    rows = total.shape[0]
    heads = total.shape[1] // head - 2

    def norm_rotate(x, gain):
        inv = lax.rsqrt(jnp.mean(x * x, axis=-1, keepdims=True) + EPSILON)
        x = x * inv * gain
        return (x * cos + pltpu.roll(x, head // 2, 1) * sin).astype(BF)

    kcol = heads * head
    kv_out[:, :head] = norm_rotate(total[:, kcol : kcol + head], kg[...])
    kv_out[:, head:] = total[:, kcol + head : kcol + 2 * head].astype(BF)
    for h in range(heads):
        q_out[h * rows : (h + 1) * rows, :] = norm_rotate(
            total[:, h * head : (h + 1) * head], qg[...]
        )


def project(chunks, w, at, acc=None, last=None, flags=()):
    count = len(chunks)
    rows, depth = chunks[0].shape
    width = w.shape[2]
    args = [*chunks, w] + ([] if acc is None else [acc]) + (list(last) if last else [])
    head = last[0].shape[1] if last else 128
    if last:
        heads = width // head - 2
        shape = [
            VMEM((heads * rows, head), BF),
            VMEM((rows, 2 * head), BF),
        ]
    else:
        shape = VMEM((rows, width), F32)
    vm = pl.BlockSpec(memory_space=VMEM)
    return pl.pallas_call(
        functools.partial(
            project_kernel, count, at, head, acc is None, last is not None, len(flags)
        ),
        in_specs=[vm] * len(args) + [pl.BlockSpec(memory_space=pl.ANY)] * len(flags),
        out_specs=[vm, vm] if last else vm,
        out_shape=shape,
        compiler_params=params(16),
        cost_estimate=pl.CostEstimate(
            flops=4 * rows * depth * count * width,
            bytes_accessed=2 * depth * count * width,
            transcendentals=0,
        ),
        name="project",
    )(*args, *flags)


def attend_kernel(layout, first, final, flags, start_s, *refs):
    n = len(layout)
    q_ref, start_ref, index_ref = refs[:3]
    kvs = refs[3 : 3 + n]
    rest = refs[3 + n :]
    if first:
        out, flag, acc = rest[flags:]
    else:
        acc_in = rest[0]
        out, flag, acc = rest[1 + flags :]
    flag[...] = jnp.zeros_like(flag)
    rows, head = q_ref.shape
    tok = start_ref.shape[0]
    heads = rows // tok
    scale = math.log2(math.e) / math.sqrt(head)
    acc[...] = jnp.zeros_like(acc) if first else acc_in[...]
    place = Place()
    own = place.seq * tok
    least = start_s[0]
    ones = jnp.ones((tok, head), BF)

    def unit(kv, bases):
        for j, base in enumerate(bases):
            at = slice(j * tok, (j + 1) * tok)
            keys = kv[at, :head]
            values = jnp.concatenate([kv[at, head:], ones], axis=1)
            col = base + lax.broadcasted_iota(jnp.int32, (tok, tok), 1)
            keep = (col >= start_ref[...]) & (col <= index_ref[...])
            for h in range(heads):
                part = slice(h * tok, (h + 1) * tok)
                s = lax.dot_general(
                    q_ref[part, :], keys, (((1,), (1,)), ((), ())), preferred_element_type=F32
                )
                p = jnp.where(keep, jnp.exp2(s * scale), 0.0).astype(BF)
                acc[part, :] += jnp.dot(p, values, preferred_element_type=F32)

    for kv, blocks in zip(kvs, layout):
        bases = [place.base(block, tok) for block in blocks]
        if blocks[0] == (0, 0):
            unit(kv, bases)
            continue
        needed = functools.reduce(
            jnp.logical_or, [(base + tok > least) & (base <= own) for base in bases]
        )
        pl.when(needed)(functools.partial(unit, kv, bases))
    if final:
        for h in range(heads):
            part = slice(h * tok, (h + 1) * tok)
            out[:, h * head : (h + 1) * head] = (acc[part, :head] / acc[part, head:]).astype(BF)
    else:
        out[...] = acc[...]


def attend(start, queries, start_col, index_col, pieces, acc=None, final=False, flags=()):
    rows, head = queries.shape
    tok = start_col.shape[0]
    kvs = [kv for kv, _ in pieces]
    layout = tuple(tuple(blocks) for _, blocks in pieces)
    first = acc is None
    args = [queries, start_col, index_col, *kvs] + ([] if first else [acc])
    if final:
        shape = VMEM((tok, rows // tok * head), BF)
    else:
        shape = VMEM((rows, 2 * head), F32)
    blocks = sum(len(blocks) for blocks in layout)
    vm = pl.BlockSpec(memory_space=VMEM)
    return pl.pallas_call(
        functools.partial(attend_kernel, layout, first, final, len(flags)),
        in_specs=[pl.BlockSpec(memory_space=pltpu.SMEM)]
        + [vm] * len(args)
        + [pl.BlockSpec(memory_space=pl.ANY)] * len(flags),
        out_specs=[vm, vm],
        out_shape=[shape, jax.ShapeDtypeStruct(FLAG, F32)],
        scratch_shapes=[pltpu.VMEM((rows, 2 * head), F32)],
        compiler_params=params(),
        cost_estimate=pl.CostEstimate(
            flops=blocks * rows * tok * head * 8,
            bytes_accessed=rows * head * 16,
            transcendentals=blocks * rows * tok,
        ),
        name="attend",
    )(start, *args, *flags)


def out_kernel(targets, a_ref, b_ref, wa, wb, *outs):
    for n, (target, out) in enumerate(zip(targets, outs)):
        s = jnp.dot(a_ref[...], wa[target], preferred_element_type=F32)
        s += jnp.dot(b_ref[...], wb[target], preferred_element_type=F32)
        out[...] = s.astype(out.dtype)


def out_project(targets, kinds, a, b, w_own, w_sib):
    rows, depth = a.shape
    cols = w_own.shape[2]
    vm = pl.BlockSpec(memory_space=VMEM)
    return pl.pallas_call(
        functools.partial(out_kernel, targets),
        in_specs=[vm] * 4,
        out_specs=[vm] * len(targets),
        out_shape=[VMEM((rows, cols), kind) for kind in kinds],
        compiler_params=params(),
        cost_estimate=pl.CostEstimate(
            flops=4 * rows * depth * cols * len(targets),
            bytes_accessed=4 * depth * cols * len(targets),
            transcendentals=0,
        ),
        name="out_project",
    )(a, b, w_own, w_sib)


def sum_kernel(mine, a, b, c, out):
    out[...] = (mine[...] + a[...].astype(F32) + b[...].astype(F32) + c[...].astype(F32)).astype(
        out.dtype
    )


def add_up(mine, others):
    vm = pl.BlockSpec(memory_space=VMEM)
    return pl.pallas_call(
        sum_kernel,
        in_specs=[vm] * 4,
        out_specs=vm,
        out_shape=jax.ShapeDtypeStruct(mine.shape, BF),
        compiler_params=params(),
        name="add_up",
    )(mine, *others)


def on_device(tokens, w_query, w_key, w_value, q_gain, k_gain, doc_lengths, w_out):
    tok, part = tokens.shape
    head = q_gain.shape[0]
    seqs, tps = lax.axis_size("seq"), lax.axis_size("tp")
    ny = 4
    nz = seqs // ny
    nx = tps // 2
    my_seq = lax.axis_index("seq")

    def sibling(a):
        return lax.ppermute(a, "tp", [(i, i ^ 1) for i in range(tps)])

    def along_x(a, d):
        return lax.ppermute(
            a,
            "tp",
            [(i, (i // 2 + (d if i % 2 == 0 else -d)) % nx * 2 + i % 2) for i in range(tps)],
        )

    def along_y(a, d):
        return lax.ppermute(a, "seq", [(i, i // ny * ny + (i + d) % ny) for i in range(seqs)])

    def along_z(a, d):
        return lax.ppermute(a, "seq", [(i, (i // ny + d) % nz * ny + i % ny) for i in range(seqs)])

    def swap_y(a, turned):
        pairs = []
        for s in range(seqs):
            for t in range(tps):
                y = s % ny
                other = y ^ 1 if t % 2 == turned else ny - 1 - y
                pairs.append((s * tps + t, (s // ny * ny + other) * tps + t))
        return lax.ppermute(a, ("seq", "tp"), pairs)

    nq, nk = w_query.shape[1], w_key.shape[1]
    arrivals = [(0, 0), (0, 1), (-1, 0), (1, 0), (1, 1), (-1, 1), (2, 0), (2, 1)]
    plan = []
    for k, shard in enumerate(arrivals):
        plan += [(0, 0, part, shard, 0, k, 0, nq), (1, 0, part, shard, 0, k, nq, nk)]
        plan += [(2, 0, part, shard, 0, k, nq + nk, nk)]
    w_in, flag_in = stage(
        [w_query, w_key, w_value], tuple(plan), [(tps, part, nq + 2 * nk)], "stage_in"
    )
    cols = w_out.shape[1] // tps
    plan = [(0, 1, cols, (d, 0), 0, k, 0, cols) for k, d in enumerate((2, 1, -1, 0))]
    plan += [(0, 1, cols, (d, 1), 1, k, 0, cols) for k, d in enumerate((2, -1, 1, 0))]
    w_own, w_send, flag_out = stage(
        [w_out], tuple(plan), [(nx, w_out.shape[0], cols)] * 2, "stage_out"
    )

    token_index = my_seq * tok + jnp.arange(tok, dtype=jnp.int32)
    start = doc_tables(doc_lengths, token_index)
    cos, sin = rope_tables(token_index - start, head)
    start_col, index_col = start[:, None], token_index[:, None]

    own = tokens
    a1, a3, a2 = along_x(own, 1), along_x(own, nx - 1), along_x(own, 2)
    b0 = sibling(own)
    acc = project([own, b0], w_in, 0)
    a1, flags = after([flag_in, flag_out], a1)
    b1 = sibling(a1)
    a3, acc, _ = after([], a3, acc)
    b3 = sibling(a3)
    a2, cos, sin, start_col, index_col, _ = after([], a2, cos, sin, start_col, index_col)
    b2 = sibling(a2)
    acc = project([a1, a3, b1, b3], w_in, 2, acc, flags=flags)
    queries, kv = project(
        [a2, b2], w_in, 6, acc, last=(cos, sin, q_gain[None, :], k_gain[None, :])
    )
    attn = (start, queries, start_col, index_col)
    r0 = kv
    r1 = along_z(r0, 1)
    r2 = along_z(r1, 1)
    r3 = along_z(r2, 1)
    r4 = along_z(r3, 1)
    x01, flag_01 = pack([r0, r1], [(0, 0), (1, 0)], tok)
    s01 = swap_y(x01, 0)
    o, flag_a = attend(*attn, [(r0, [(0, 0)]), (r1, [(1, 0)])], flags=[flag_01])
    x_one, flag_1 = pack([r1, s01], [(0, 0), (1, 1)], tok)
    near_one = swap_y(x_one, 1)
    o, flag_b = attend(*attn, [(s01, [(0, 1), (1, 1)]), (r2, [(2, 0)])], o, flags=[flag_1])
    x23, flag_23 = pack([r2, r3], [(0, 0), (1, 0)], tok)
    s23 = swap_y(x23, 0)
    s4 = swap_y(r4, 0)
    x_two, flag_2 = pack(
        [r2, s23, r3], [(0, 0), (1, 0), (2, 0), (1, 1)], tok, flags=[hold(r4)]
    )
    near_two = swap_y(x_two, 1)
    o, flag_c = attend(
        *attn,
        [(near_one, [(1, 2), (1, 3)]), (r3, [(3, 0)]), (s23, [(2, 1), (3, 1)])],
        o,
        flags=[flag_2],
    )
    x_last, flag_l = pack(
        [r0, r4, s01, s4], [(0, (0, 0), (1, 0)), (1, (2, 0), (3, 0))], tok, flags=[hold(s4)]
    )
    last = swap_y(x_last, 1)
    w_send, _ = after([flag_l], w_send)
    w_sib, flag_w = fetch(sibling(w_send))
    o, _ = attend(
        *attn,
        [(near_two, [(2, 2), (2, 3), (3, 2), (3, 3)]), (r4, [(4, 0)]), (s4, [(4, 1)])],
        o,
        flags=[flag_l, flag_w, hold(near_two)],
    )
    attended, _ = attend(*attn, [(last, [(None, 2), (None, 3)])], o, final=True)

    attended_sib = sibling(attended)
    (p2,) = out_project((0,), (BF,), attended, attended_sib, w_own, w_sib)
    t2 = along_x(p2, 2)
    p1, p3 = out_project((1, 2), (BF, BF), attended, attended_sib, w_own, w_sib)
    t1 = along_x(p1, 1)
    t3 = along_x(p3, nx - 1)
    (mine,) = out_project((3,), (F32,), attended, attended_sib, w_own, w_sib)
    return add_up(mine, [t1, t2, t3])


def solution(mesh):
    return jax.shard_map(
        on_device,
        mesh=mesh,
        in_specs=(
            P("seq", "tp"),
            P(None, "tp"),
            P(None, "tp"),
            P(None, "tp"),
            P(),
            P(),
            P(),
            P("tp", None),
        ),
        out_specs=P("seq", "tp"),
        check_vma=False,
    )
```

```python
import functools
import math

import jax
import jax.numpy as jnp
from jax import lax
from jax.experimental import pallas as pl
from jax.experimental.pallas import tpu as pltpu
from jax.sharding import PartitionSpec as P

EPSILON = 1e-06
ROPE_THETA = 1000000.0
BF = jnp.bfloat16
F32 = jnp.float32
VMEM = pltpu.VMEM
MIB = 1024 * 1024


def params(limit=10):
    return pltpu.CompilerParams(vmem_limit_bytes=limit * MIB)


def doc_tables(doc_lengths, token_index):
    doc_ends = jnp.cumsum(doc_lengths)
    passed = (token_index[:, None] >= doc_ends[None, :]).astype(jnp.int32)
    return jnp.sum(passed * doc_lengths[None, :], axis=1)


def rope_tables(position, head_width):
    half = head_width // 2
    frequency = ROPE_THETA ** (-(jnp.arange(half, dtype=F32) * 2.0 / head_width))
    angles = position.astype(F32)[:, None] * frequency[None, :]
    cos, sin = jnp.cos(angles), jnp.sin(angles)
    return jnp.concatenate([cos, cos], axis=1), jnp.concatenate([-sin, sin], axis=1)


NX, NY = 4, 4


class Place:
    def __init__(self):
        seq, tp = lax.axis_index("seq"), lax.axis_index("tp")
        self.seq, self.z, self.y = seq, seq // NY, lax.rem(seq, NY)
        self.x, self.c = tp // 2, lax.rem(tp, 2)

        def flip(a):
            return a + 1 - 2 * lax.rem(a, 2)

        even = self.c == 0
        self.y1 = jnp.where(even, flip(self.y), NY - 1 - self.y)
        self.y2 = jnp.where(even, NY - 1 - self.y, flip(self.y))
        self.y3 = jnp.where(even, flip(self.y2), NY - 1 - self.y2)

    def chip(self, turn):
        return lax.rem(self.x + NX + turn * (1 - 2 * self.c), NX)

    def part(self, turn, other):
        return 2 * self.chip(turn) + (1 - self.c if other else self.c)

    def base(self, block, tok):
        back, who = block
        if back is None:
            wraps = self.y < who
            back, y = jnp.where(wraps, 4, 0), self.y - who + jnp.where(wraps, NY, 0)
        else:
            y = (self.y, self.y1, self.y2, self.y3)[who]
        return ((self.z - back) * NY + y) * tok


def stage_kernel(plan, sources, *refs):
    ins, rest = refs[:sources], refs[sources:]
    outs, flag, sem = rest[:-2], rest[-2], rest[-1]
    place = Place()
    copies = []
    for n, (src, axis, size, (turn, other), dst, row, col, cols) in enumerate(plan):
        cut = pl.ds(pl.multiple_of(place.part(turn, other) * size, size), size)
        view = ins[src].at[cut, :] if axis == 0 else ins[src].at[:, cut]
        copies.append(
            pltpu.make_async_copy(view, outs[dst].at[row, :, col : col + cols], sem.at[n])
        )
    for c in copies:
        c.start()
    flag[...] = jnp.zeros_like(flag)
    for c in copies:
        c.wait()


FLAG = (8, 128)


def fetch_kernel(src, *refs):
    out, flag, sem = refs[-3:]
    copy = pltpu.make_async_copy(src, out, sem)
    copy.start()
    flag[...] = jnp.zeros_like(flag)
    copy.wait()


def fetch(a, flags=()):
    vm = pl.BlockSpec(memory_space=VMEM)
    return pl.pallas_call(
        fetch_kernel,
        in_specs=[pl.BlockSpec(memory_space=pl.ANY)] * (1 + len(flags)),
        out_specs=[vm, vm],
        out_shape=[VMEM(a.shape, a.dtype), jax.ShapeDtypeStruct(FLAG, F32)],
        scratch_shapes=[pltpu.SemaphoreType.DMA],
        compiler_params=params(),
        name="fetch",
    )(a, *flags)


def stage(arrays, plan, shapes, name):
    vm = pl.BlockSpec(memory_space=VMEM)
    return pl.pallas_call(
        functools.partial(stage_kernel, plan, len(arrays)),
        in_specs=[pl.BlockSpec(memory_space=pltpu.HBM)] * len(arrays),
        out_specs=[vm] * (len(shapes) + 1),
        out_shape=[VMEM(shape, BF) for shape in shapes] + [jax.ShapeDtypeStruct(FLAG, F32)],
        scratch_shapes=[pltpu.SemaphoreType.DMA((len(plan),))],
        compiler_params=params(14),
        cost_estimate=pl.CostEstimate(
            flops=0, bytes_accessed=sum(4 * math.prod(shape) for shape in shapes), transcendentals=0
        ),
        name=name,
    )(*[pltpu.with_memory_space_constraint(a, pltpu.HBM) for a in arrays])


def after(flags, *arrays):
    out = lax.optimization_barrier((*arrays, *flags))
    return (*out[: len(arrays)], list(out[len(arrays) :]))


def hold_kernel(*refs):
    refs[-1][...] = jnp.zeros(FLAG, F32)


def hold(*arrays, cost=20):
    return pl.pallas_call(
        hold_kernel,
        in_specs=[pl.BlockSpec(memory_space=pl.ANY)] * len(arrays),
        out_specs=pl.BlockSpec(memory_space=VMEM),
        out_shape=jax.ShapeDtypeStruct(FLAG, F32),
        compiler_params=params(),
        cost_estimate=pl.CostEstimate(flops=cost * 10**9, bytes_accessed=4096, transcendentals=0),
        name="hold",
    )(*arrays)


def pack_kernel(pieces, tok, count, *refs):
    ins, out, flag = refs[:count], refs[-2], refs[-1]
    flag[...] = jnp.zeros_like(flag)
    for n, piece in enumerate(pieces):
        to = slice(n * tok, (n + 1) * tok)
        src, at = piece
        out[to, :] = ins[src][at * tok : (at + 1) * tok, :]


def pack(arrays, pieces, tok, flags=()):
    vm = pl.BlockSpec(memory_space=VMEM)
    count = len(arrays)
    return pl.pallas_call(
        functools.partial(pack_kernel, tuple(pieces), tok, count),
        in_specs=[vm] * count + [pl.BlockSpec(memory_space=pl.ANY)] * len(flags),
        out_specs=[vm, vm],
        out_shape=[
            VMEM((len(pieces) * tok, arrays[0].shape[1]), BF),
            jax.ShapeDtypeStruct(FLAG, F32),
        ],
        compiler_params=params(),
        name="pack",
    )(*arrays, *flags)


def mix_kernel(own, far, *refs):
    outs, flag = refs[-NY:-1], refs[-1]
    flag[...] = jnp.zeros_like(flag)
    place = Place()
    for e, out in enumerate(outs, 1):
        here = place.y + e < NY

        def put(src, out=out):
            out[...] = src[...]

        pl.when(here)(functools.partial(put, own))
        pl.when(jnp.logical_not(here))(functools.partial(put, far))


def mixes(own, far, flags=()):
    vm = pl.BlockSpec(memory_space=VMEM)
    return pl.pallas_call(
        mix_kernel,
        in_specs=[vm] * 2 + [pl.BlockSpec(memory_space=pl.ANY)] * len(flags),
        out_specs=[vm] * NY,
        out_shape=[VMEM(own.shape, BF)] * (NY - 1) + [jax.ShapeDtypeStruct(FLAG, F32)],
        compiler_params=params(),
        name="mixes",
    )(own, far, *flags)


def project_kernel(count, at, head, first, last, flags, *refs):
    chunks, w = refs[:count], refs[count]
    rest = refs[count + 1 :]
    outs = 2 if last else 1
    rest = rest[: len(rest) - flags - outs] + rest[len(rest) - outs :]
    total = None
    for k in range(count):
        prod = jnp.dot(chunks[k][...], w[at + k], preferred_element_type=F32)
        total = prod if total is None else total + prod
    if not first:
        total = total + rest[0][...]
        rest = rest[1:]
    if not last:
        rest[0][...] = total
        return
    cos_ref, sin_ref, qg, kg, q_out, kv_out = rest
    cos = cos_ref[...]
    sin = sin_ref[...]
    rows = total.shape[0]
    heads = total.shape[1] // head - 2

    def norm_rotate(x, gain):
        inv = lax.rsqrt(jnp.mean(x * x, axis=-1, keepdims=True) + EPSILON)
        x = x * inv * gain
        return (x * cos + pltpu.roll(x, head // 2, 1) * sin).astype(BF)

    kcol = heads * head
    kv_out[:, :head] = norm_rotate(total[:, kcol : kcol + head], kg[...])
    kv_out[:, head:] = total[:, kcol + head : kcol + 2 * head].astype(BF)
    for h in range(heads):
        q_out[h * rows : (h + 1) * rows, :] = norm_rotate(
            total[:, h * head : (h + 1) * head], qg[...]
        )


def project(chunks, w, at, acc=None, last=None, flags=()):
    count = len(chunks)
    rows, depth = chunks[0].shape
    width = w.shape[2]
    args = [*chunks, w] + ([] if acc is None else [acc]) + (list(last) if last else [])
    head = last[0].shape[1] if last else 128
    if last:
        heads = width // head - 2
        shape = [
            VMEM((heads * rows, head), BF),
            VMEM((rows, 2 * head), BF),
        ]
    else:
        shape = VMEM((rows, width), F32)
    vm = pl.BlockSpec(memory_space=VMEM)
    return pl.pallas_call(
        functools.partial(
            project_kernel, count, at, head, acc is None, last is not None, len(flags)
        ),
        in_specs=[vm] * len(args) + [pl.BlockSpec(memory_space=pl.ANY)] * len(flags),
        out_specs=[vm, vm] if last else vm,
        out_shape=shape,
        compiler_params=params(16),
        cost_estimate=pl.CostEstimate(
            flops=4 * rows * depth * count * width,
            bytes_accessed=2 * depth * count * width,
            transcendentals=0,
        ),
        name="project",
    )(*args, *flags)


def attend_kernel(layout, first, final, flags, start_s, *refs):
    n = len(layout)
    q_ref, start_ref, index_ref = refs[:3]
    kvs = refs[3 : 3 + n]
    rest = refs[3 + n :]
    if first:
        out, flag, acc = rest[flags:]
    else:
        acc_in = rest[0]
        out, flag, acc = rest[1 + flags :]
    flag[...] = jnp.zeros_like(flag)
    rows, head = q_ref.shape
    tok = start_ref.shape[0]
    heads = rows // tok
    scale = math.log2(math.e) / math.sqrt(head)
    acc[...] = jnp.zeros_like(acc) if first else acc_in[...]
    place = Place()
    own = place.seq * tok
    least = start_s[0]
    ones = jnp.ones((tok, head), BF)

    def unit(kv, bases):
        for j, base in enumerate(bases):
            at = slice(j * tok, (j + 1) * tok)
            keys = kv[at, :head]
            values = jnp.concatenate([kv[at, head:], ones], axis=1)
            col = base + lax.broadcasted_iota(jnp.int32, (tok, tok), 1)
            keep = (col >= start_ref[...]) & (col <= index_ref[...])
            for h in range(heads):
                part = slice(h * tok, (h + 1) * tok)
                s = lax.dot_general(
                    q_ref[part, :], keys, (((1,), (1,)), ((), ())), preferred_element_type=F32
                )
                p = jnp.where(keep, jnp.exp2(s * scale), 0.0).astype(BF)
                acc[part, :] += jnp.dot(p, values, preferred_element_type=F32)

    for kv, blocks in zip(kvs, layout):
        bases = [place.base(block, tok) for block in blocks]
        if blocks[0] == (0, 0):
            unit(kv, bases)
            continue
        needed = functools.reduce(
            jnp.logical_or, [(base + tok > least) & (base <= own) for base in bases]
        )
        pl.when(needed)(functools.partial(unit, kv, bases))
    if final:
        for h in range(heads):
            part = slice(h * tok, (h + 1) * tok)
            out[:, h * head : (h + 1) * head] = (acc[part, :head] / acc[part, head:]).astype(BF)
    else:
        out[...] = acc[...]


def attend(start, queries, start_col, index_col, pieces, acc=None, final=False, flags=()):
    rows, head = queries.shape
    tok = start_col.shape[0]
    kvs = [kv for kv, _ in pieces]
    layout = tuple(tuple(blocks) for _, blocks in pieces)
    first = acc is None
    args = [queries, start_col, index_col, *kvs] + ([] if first else [acc])
    if final:
        shape = VMEM((tok, rows // tok * head), BF)
    else:
        shape = VMEM((rows, 2 * head), F32)
    blocks = sum(len(blocks) for blocks in layout)
    vm = pl.BlockSpec(memory_space=VMEM)
    return pl.pallas_call(
        functools.partial(attend_kernel, layout, first, final, len(flags)),
        in_specs=[pl.BlockSpec(memory_space=pltpu.SMEM)]
        + [vm] * len(args)
        + [pl.BlockSpec(memory_space=pl.ANY)] * len(flags),
        out_specs=[vm, vm],
        out_shape=[shape, jax.ShapeDtypeStruct(FLAG, F32)],
        scratch_shapes=[pltpu.VMEM((rows, 2 * head), F32)],
        compiler_params=params(),
        cost_estimate=pl.CostEstimate(
            flops=blocks * rows * tok * head * 8,
            bytes_accessed=rows * head * 16,
            transcendentals=blocks * rows * tok,
        ),
        name="attend",
    )(start, *args, *flags)


def out_kernel(targets, a_ref, b_ref, wa, wb, *outs):
    for n, (target, out) in enumerate(zip(targets, outs)):
        s = jnp.dot(a_ref[...], wa[target], preferred_element_type=F32)
        s += jnp.dot(b_ref[...], wb[target], preferred_element_type=F32)
        out[...] = s.astype(out.dtype)


def out_project(targets, kinds, a, b, w_own, w_sib):
    rows, depth = a.shape
    cols = w_own.shape[2]
    vm = pl.BlockSpec(memory_space=VMEM)
    return pl.pallas_call(
        functools.partial(out_kernel, targets),
        in_specs=[vm] * 4,
        out_specs=[vm] * len(targets),
        out_shape=[VMEM((rows, cols), kind) for kind in kinds],
        compiler_params=params(),
        cost_estimate=pl.CostEstimate(
            flops=4 * rows * depth * cols * len(targets),
            bytes_accessed=4 * depth * cols * len(targets),
            transcendentals=0,
        ),
        name="out_project",
    )(a, b, w_own, w_sib)


def sum_kernel(mine, a, b, c, out):
    out[...] = (mine[...] + a[...].astype(F32) + b[...].astype(F32) + c[...].astype(F32)).astype(
        out.dtype
    )


def add_up(mine, others):
    vm = pl.BlockSpec(memory_space=VMEM)
    return pl.pallas_call(
        sum_kernel,
        in_specs=[vm] * 4,
        out_specs=vm,
        out_shape=jax.ShapeDtypeStruct(mine.shape, BF),
        compiler_params=params(),
        name="add_up",
    )(mine, *others)


def on_device(tokens, w_query, w_key, w_value, q_gain, k_gain, doc_lengths, w_out):
    tok, part = tokens.shape
    head = q_gain.shape[0]
    seqs, tps = lax.axis_size("seq"), lax.axis_size("tp")
    ny = 4
    nz = seqs // ny
    nx = tps // 2
    my_seq = lax.axis_index("seq")

    def sibling(a):
        return lax.ppermute(a, "tp", [(i, i ^ 1) for i in range(tps)])

    def along_x(a, d):
        return lax.ppermute(
            a,
            "tp",
            [(i, (i // 2 + (d if i % 2 == 0 else -d)) % nx * 2 + i % 2) for i in range(tps)],
        )

    def along_y(a, d):
        return lax.ppermute(a, "seq", [(i, i // ny * ny + (i + d) % ny) for i in range(seqs)])

    def along_y(a, d):
        return lax.ppermute(a, "seq", [(i, i // ny * ny + (i + d) % ny) for i in range(seqs)])

    def along_z(a, d):
        return lax.ppermute(a, "seq", [(i, (i // ny + d) % nz * ny + i % ny) for i in range(seqs)])

    def swap_y(a, turned):
        pairs = []
        for s in range(seqs):
            for t in range(tps):
                y = s % ny
                other = y ^ 1 if t % 2 == turned else ny - 1 - y
                pairs.append((s * tps + t, (s // ny * ny + other) * tps + t))
        return lax.ppermute(a, ("seq", "tp"), pairs)

    nq, nk = w_query.shape[1], w_key.shape[1]
    arrivals = [(0, 0), (0, 1), (-1, 0), (1, 0), (1, 1), (-1, 1), (2, 0), (2, 1)]
    plan = []
    for k, shard in enumerate(arrivals):
        plan += [(0, 0, part, shard, 0, k, 0, nq), (1, 0, part, shard, 0, k, nq, nk)]
        plan += [(2, 0, part, shard, 0, k, nq + nk, nk)]
    w_in, flag_in = stage(
        [w_query, w_key, w_value], tuple(plan), [(tps, part, nq + 2 * nk)], "stage_in"
    )
    cols = w_out.shape[1] // tps
    plan = [(0, 1, cols, (d, 0), 0, k, 0, cols) for k, d in enumerate((2, 1, -1, 0))]
    plan += [(0, 1, cols, (d, 1), 1, k, 0, cols) for k, d in enumerate((2, -1, 1, 0))]
    w_own, w_send, flag_out = stage(
        [w_out], tuple(plan), [(nx, w_out.shape[0], cols)] * 2, "stage_out"
    )

    token_index = my_seq * tok + jnp.arange(tok, dtype=jnp.int32)
    start = doc_tables(doc_lengths, token_index)
    cos, sin = rope_tables(token_index - start, head)
    start_col, index_col = start[:, None], token_index[:, None]

    own = tokens
    a1, a3, a2 = along_x(own, 1), along_x(own, nx - 1), along_x(own, 2)
    b0 = sibling(own)
    acc = project([own, b0], w_in, 0)
    a1, flags = after([flag_in, flag_out], a1)
    b1 = sibling(a1)
    a3, acc, _ = after([], a3, acc)
    b3 = sibling(a3)
    a2, cos, sin, start_col, index_col, _ = after([], a2, cos, sin, start_col, index_col)
    b2 = sibling(a2)
    acc = project([a1, a3, b1, b3], w_in, 2, acc, flags=flags)
    queries, kv = project(
        [a2, b2], w_in, 6, acc, last=(cos, sin, q_gain[None, :], k_gain[None, :])
    )
    attn = (start, queries, start_col, index_col)
    r0 = kv
    r1 = along_z(r0, 1)
    r2 = along_z(r1, 1)
    r3 = along_z(r2, 1)
    r4 = along_z(r3, 1)
    s1, s2, s3 = swap_y(r1, 0), swap_y(r2, 0), swap_y(r3, 0)
    w_sib = sibling(w_send)
    got = hold(w_sib, cost=0)
    o, flag_a = attend(*attn, [(r0, [(0, 0)])])
    x_one, flag_1 = pack([r1, s1], [(0, 0), (1, 0)], tok)
    near_one = swap_y(x_one, 1)
    o, flag_b = attend(*attn, [(r1, [(1, 0)]), (r2, [(2, 0)])], o, flags=[flag_1])
    x_two, flag_2 = pack([r2, s2], [(0, 0), (1, 0)], tok, flags=[hold(r3), got, flag_b])
    near_two = swap_y(x_two, 1)
    x1, x2, x3, flag_m = mixes(r0, r4, flags=[hold(r4), flag_2])
    mixed = [(along_y((x1, x2, x3)[e - 1], e), [(None, e)]) for e in (2, 1, 3)]
    x_three, flag_3 = pack([r3, s3], [(0, 0), (1, 0)], tok, flags=[flag_m])
    near_three = swap_y(x_three, 1)
    o, flag_c = attend(
        *attn,
        [(s1, [(1, 1)]), (s2, [(2, 1)]), (near_one, [(1, 2), (1, 3)]), (r3, [(3, 0)])],
        o,
        flags=[flag_3],
    )
    w_sib, flag_w = fetch(w_sib, [flag_3])
    o, flag_d = attend(
        *attn, [(near_two, [(2, 2), (2, 3)]), (s3, [(3, 1)]), (r4, [(4, 0)])], o
    )
    attended, _ = attend(
        *attn,
        [(near_three, [(3, 2), (3, 3)]), *mixed],
        o,
        final=True,
        flags=[flag_w, hold(*[m for m, _ in mixed], flag_d, cost=2)],
    )

    attended_sib = sibling(attended)
    (p2,) = out_project((0,), (BF,), attended, attended_sib, w_own, w_sib)
    t2 = along_x(p2, 2)
    p1, p3 = out_project((1, 2), (BF, BF), attended, attended_sib, w_own, w_sib)
    t1 = along_x(p1, 1)
    t3 = along_x(p3, nx - 1)
    (mine,) = out_project((3,), (F32,), attended, attended_sib, w_own, w_sib)
    return add_up(mine, [t1, t2, t3])


def solution(mesh):
    return jax.shard_map(
        on_device,
        mesh=mesh,
        in_specs=(
            P("seq", "tp"),
            P(None, "tp"),
            P(None, "tp"),
            P(None, "tp"),
            P(),
            P(),
            P(),
            P("tp", None),
        ),
        out_specs=P("seq", "tp"),
        check_vma=False,
    )
```

```python
import functools
import math

import jax
import jax.numpy as jnp
from jax import lax
from jax.experimental import pallas as pl
from jax.experimental.pallas import tpu as pltpu
from jax.sharding import PartitionSpec as P

EPSILON = 1e-06
ROPE_THETA = 1000000.0
BF = jnp.bfloat16
F32 = jnp.float32
VMEM = pltpu.VMEM
MIB = 1024 * 1024


def params(limit=10):
    return pltpu.CompilerParams(vmem_limit_bytes=limit * MIB)


def doc_tables(doc_lengths, token_index):
    doc_ends = jnp.cumsum(doc_lengths)
    passed = (token_index[:, None] >= doc_ends[None, :]).astype(jnp.int32)
    return jnp.sum(passed * doc_lengths[None, :], axis=1)


def rope_tables(position, head_width):
    half = head_width // 2
    frequency = ROPE_THETA ** (-(jnp.arange(half, dtype=F32) * 2.0 / head_width))
    angles = position.astype(F32)[:, None] * frequency[None, :]
    cos, sin = jnp.cos(angles), jnp.sin(angles)
    return jnp.concatenate([cos, cos], axis=1), jnp.concatenate([-sin, sin], axis=1)


NX, NY = 4, 4


class Place:
    def __init__(self):
        seq, tp = lax.axis_index("seq"), lax.axis_index("tp")
        self.seq, self.z, self.y = seq, seq // NY, lax.rem(seq, NY)
        self.x, self.c = tp // 2, lax.rem(tp, 2)

        def flip(a):
            return a + 1 - 2 * lax.rem(a, 2)

        even = self.c == 0
        self.y1 = jnp.where(even, flip(self.y), NY - 1 - self.y)
        self.y2 = jnp.where(even, NY - 1 - self.y, flip(self.y))
        self.y3 = jnp.where(even, flip(self.y2), NY - 1 - self.y2)

    def chip(self, turn):
        return lax.rem(self.x + NX + turn * (1 - 2 * self.c), NX)

    def part(self, turn, other):
        return 2 * self.chip(turn) + (1 - self.c if other else self.c)

    def base(self, block, tok):
        back, who = block
        if back is None:
            wraps = self.y < who
            back, y = jnp.where(wraps, 4, 0), self.y - who + jnp.where(wraps, NY, 0)
        else:
            y = (self.y, self.y1, self.y2, self.y3)[who]
        return ((self.z - back) * NY + y) * tok


def stage_kernel(plan, sources, *refs):
    ins, rest = refs[:sources], refs[sources:]
    outs, flag, sem = rest[:-2], rest[-2], rest[-1]
    place = Place()
    copies = []
    for n, (src, axis, size, (turn, other), dst, row, col, cols) in enumerate(plan):
        cut = pl.ds(pl.multiple_of(place.part(turn, other) * size, size), size)
        view = ins[src].at[cut, :] if axis == 0 else ins[src].at[:, cut]
        copies.append(
            pltpu.make_async_copy(view, outs[dst].at[row, :, col : col + cols], sem.at[n])
        )
    for c in copies:
        c.start()
    flag[...] = jnp.zeros_like(flag)
    for c in copies:
        c.wait()


FLAG = (8, 128)


def fetch_kernel(src, *refs):
    out, flag, sem = refs[-3:]
    copy = pltpu.make_async_copy(src, out, sem)
    copy.start()
    flag[...] = jnp.zeros_like(flag)
    copy.wait()


def fetch(a, flags=()):
    vm = pl.BlockSpec(memory_space=VMEM)
    return pl.pallas_call(
        fetch_kernel,
        in_specs=[pl.BlockSpec(memory_space=pl.ANY)] * (1 + len(flags)),
        out_specs=[vm, vm],
        out_shape=[VMEM(a.shape, a.dtype), jax.ShapeDtypeStruct(FLAG, F32)],
        scratch_shapes=[pltpu.SemaphoreType.DMA],
        compiler_params=params(),
        name="fetch",
    )(a, *flags)


def stage(arrays, plan, shapes, name):
    vm = pl.BlockSpec(memory_space=VMEM)
    return pl.pallas_call(
        functools.partial(stage_kernel, plan, len(arrays)),
        in_specs=[pl.BlockSpec(memory_space=pltpu.HBM)] * len(arrays),
        out_specs=[vm] * (len(shapes) + 1),
        out_shape=[VMEM(shape, BF) for shape in shapes] + [jax.ShapeDtypeStruct(FLAG, F32)],
        scratch_shapes=[pltpu.SemaphoreType.DMA((len(plan),))],
        compiler_params=params(14),
        cost_estimate=pl.CostEstimate(
            flops=0, bytes_accessed=sum(4 * math.prod(shape) for shape in shapes), transcendentals=0
        ),
        name=name,
    )(*[pltpu.with_memory_space_constraint(a, pltpu.HBM) for a in arrays])


def after(flags, *arrays):
    out = lax.optimization_barrier((*arrays, *flags))
    return (*out[: len(arrays)], list(out[len(arrays) :]))


def hold_kernel(*refs):
    refs[-1][...] = jnp.zeros(FLAG, F32)


def hold(*arrays, cost=20):
    return pl.pallas_call(
        hold_kernel,
        in_specs=[pl.BlockSpec(memory_space=pl.ANY)] * len(arrays),
        out_specs=pl.BlockSpec(memory_space=VMEM),
        out_shape=jax.ShapeDtypeStruct(FLAG, F32),
        compiler_params=params(),
        cost_estimate=pl.CostEstimate(flops=cost * 10**9, bytes_accessed=4096, transcendentals=0),
        name="hold",
    )(*arrays)


def pack_kernel(pieces, tok, count, *refs):
    ins, out, flag = refs[:count], refs[-2], refs[-1]
    flag[...] = jnp.zeros_like(flag)
    for n, piece in enumerate(pieces):
        to = slice(n * tok, (n + 1) * tok)
        src, at = piece
        out[to, :] = ins[src][at * tok : (at + 1) * tok, :]


def pack(arrays, pieces, tok, flags=()):
    vm = pl.BlockSpec(memory_space=VMEM)
    count = len(arrays)
    return pl.pallas_call(
        functools.partial(pack_kernel, tuple(pieces), tok, count),
        in_specs=[vm] * count + [pl.BlockSpec(memory_space=pl.ANY)] * len(flags),
        out_specs=[vm, vm],
        out_shape=[
            VMEM((len(pieces) * tok, arrays[0].shape[1]), BF),
            jax.ShapeDtypeStruct(FLAG, F32),
        ],
        compiler_params=params(),
        name="pack",
    )(*arrays, *flags)


def mix_kernel(own, far, *refs):
    outs, flag = refs[-NY:-1], refs[-1]
    flag[...] = jnp.zeros_like(flag)
    place = Place()
    for e, out in enumerate(outs, 1):
        here = place.y + e < NY

        def put(src, out=out):
            out[...] = src[...]

        pl.when(here)(functools.partial(put, own))
        pl.when(jnp.logical_not(here))(functools.partial(put, far))


def mixes(own, far, flags=()):
    vm = pl.BlockSpec(memory_space=VMEM)
    return pl.pallas_call(
        mix_kernel,
        in_specs=[vm] * 2 + [pl.BlockSpec(memory_space=pl.ANY)] * len(flags),
        out_specs=[vm] * NY,
        out_shape=[VMEM(own.shape, BF)] * (NY - 1) + [jax.ShapeDtypeStruct(FLAG, F32)],
        compiler_params=params(),
        name="mixes",
    )(own, far, *flags)


def project_kernel(count, at, head, first, last, flags, *refs):
    chunks, w = refs[:count], refs[count]
    rest = refs[count + 1 :]
    outs = 2 if last else 1
    rest = rest[: len(rest) - flags - outs] + rest[len(rest) - outs :]
    total = None
    for k in range(count):
        prod = jnp.dot(chunks[k][...], w[at + k], preferred_element_type=F32)
        total = prod if total is None else total + prod
    if not first:
        total = total + rest[0][...]
        rest = rest[1:]
    if not last:
        rest[0][...] = total
        return
    cos_ref, sin_ref, qg, kg, q_out, kv_out = rest
    cos = cos_ref[...]
    sin = sin_ref[...]
    rows = total.shape[0]
    heads = total.shape[1] // head - 2

    def norm_rotate(x, gain):
        inv = lax.rsqrt(jnp.mean(x * x, axis=-1, keepdims=True) + EPSILON)
        x = x * inv * gain
        return (x * cos + pltpu.roll(x, head // 2, 1) * sin).astype(BF)

    kcol = heads * head
    kv_out[:, :head] = norm_rotate(total[:, kcol : kcol + head], kg[...])
    kv_out[:, head:] = total[:, kcol + head : kcol + 2 * head].astype(BF)
    for h in range(heads):
        q_out[h * rows : (h + 1) * rows, :] = norm_rotate(
            total[:, h * head : (h + 1) * head], qg[...]
        )


def project(chunks, w, at, acc=None, last=None, flags=()):
    count = len(chunks)
    rows, depth = chunks[0].shape
    width = w.shape[2]
    args = [*chunks, w] + ([] if acc is None else [acc]) + (list(last) if last else [])
    head = last[0].shape[1] if last else 128
    if last:
        heads = width // head - 2
        shape = [
            VMEM((heads * rows, head), BF),
            VMEM((rows, 2 * head), BF),
        ]
    else:
        shape = VMEM((rows, width), F32)
    vm = pl.BlockSpec(memory_space=VMEM)
    return pl.pallas_call(
        functools.partial(
            project_kernel, count, at, head, acc is None, last is not None, len(flags)
        ),
        in_specs=[vm] * len(args) + [pl.BlockSpec(memory_space=pl.ANY)] * len(flags),
        out_specs=[vm, vm] if last else vm,
        out_shape=shape,
        compiler_params=params(16),
        cost_estimate=pl.CostEstimate(
            flops=4 * rows * depth * count * width,
            bytes_accessed=2 * depth * count * width,
            transcendentals=0,
        ),
        name="project",
    )(*args, *flags)


def attend_kernel(layout, first, final, flags, start_s, *refs):
    n = len(layout)
    q_ref, start_ref, index_ref = refs[:3]
    kvs = refs[3 : 3 + n]
    rest = refs[3 + n :]
    if first:
        out, flag, acc = rest[flags:]
    else:
        acc_in = rest[0]
        out, flag, acc = rest[1 + flags :]
    flag[...] = jnp.zeros_like(flag)
    rows, head = q_ref.shape
    tok = start_ref.shape[0]
    heads = rows // tok
    scale = math.log2(math.e) / math.sqrt(head)
    acc[...] = jnp.zeros_like(acc) if first else acc_in[...]
    place = Place()
    own = place.seq * tok
    least = start_s[0]
    ones = jnp.ones((tok, head), BF)

    def unit(kv, bases):
        for j, base in enumerate(bases):
            at = slice(j * tok, (j + 1) * tok)
            keys = kv[at, :head]
            values = jnp.concatenate([kv[at, head:], ones], axis=1)
            col = base + lax.broadcasted_iota(jnp.int32, (tok, tok), 1)
            keep = (col >= start_ref[...]) & (col <= index_ref[...])
            for h in range(heads):
                part = slice(h * tok, (h + 1) * tok)
                s = lax.dot_general(
                    q_ref[part, :], keys, (((1,), (1,)), ((), ())), preferred_element_type=F32
                )
                p = jnp.where(keep, jnp.exp2(s * scale), 0.0).astype(BF)
                acc[part, :] += jnp.dot(p, values, preferred_element_type=F32)

    for kv, blocks in zip(kvs, layout):
        bases = [place.base(block, tok) for block in blocks]
        if blocks[0] == (0, 0):
            unit(kv, bases)
            continue
        needed = functools.reduce(
            jnp.logical_or, [(base + tok > least) & (base <= own) for base in bases]
        )
        pl.when(needed)(functools.partial(unit, kv, bases))
    if final:
        for h in range(heads):
            part = slice(h * tok, (h + 1) * tok)
            out[:, h * head : (h + 1) * head] = (acc[part, :head] / acc[part, head:]).astype(BF)
    else:
        out[...] = acc[...]


def attend(start, queries, start_col, index_col, pieces, acc=None, final=False, flags=()):
    rows, head = queries.shape
    tok = start_col.shape[0]
    kvs = [kv for kv, _ in pieces]
    layout = tuple(tuple(blocks) for _, blocks in pieces)
    first = acc is None
    args = [queries, start_col, index_col, *kvs] + ([] if first else [acc])
    if final:
        shape = VMEM((tok, rows // tok * head), BF)
    else:
        shape = VMEM((rows, 2 * head), F32)
    blocks = sum(len(blocks) for blocks in layout)
    vm = pl.BlockSpec(memory_space=VMEM)
    return pl.pallas_call(
        functools.partial(attend_kernel, layout, first, final, len(flags)),
        in_specs=[pl.BlockSpec(memory_space=pltpu.SMEM)]
        + [vm] * len(args)
        + [pl.BlockSpec(memory_space=pl.ANY)] * len(flags),
        out_specs=[vm, vm],
        out_shape=[shape, jax.ShapeDtypeStruct(FLAG, F32)],
        scratch_shapes=[pltpu.VMEM((rows, 2 * head), F32)],
        compiler_params=params(),
        cost_estimate=pl.CostEstimate(
            flops=blocks * rows * tok * head * 8,
            bytes_accessed=rows * head * 16,
            transcendentals=blocks * rows * tok,
        ),
        name="attend",
    )(start, *args, *flags)


def out_kernel(targets, a_ref, b_ref, wa, wb, *outs):
    for n, (target, out) in enumerate(zip(targets, outs)):
        s = jnp.dot(a_ref[...], wa[target], preferred_element_type=F32)
        s += jnp.dot(b_ref[...], wb[target], preferred_element_type=F32)
        out[...] = s.astype(out.dtype)


def out_project(targets, kinds, a, b, w_own, w_sib):
    rows, depth = a.shape
    cols = w_own.shape[2]
    vm = pl.BlockSpec(memory_space=VMEM)
    return pl.pallas_call(
        functools.partial(out_kernel, targets),
        in_specs=[vm] * 4,
        out_specs=[vm] * len(targets),
        out_shape=[VMEM((rows, cols), kind) for kind in kinds],
        compiler_params=params(),
        cost_estimate=pl.CostEstimate(
            flops=4 * rows * depth * cols * len(targets),
            bytes_accessed=4 * depth * cols * len(targets),
            transcendentals=0,
        ),
        name="out_project",
    )(a, b, w_own, w_sib)


def sum_kernel(mine, a, b, c, out):
    out[...] = (mine[...] + a[...].astype(F32) + b[...].astype(F32) + c[...].astype(F32)).astype(
        out.dtype
    )


def add_up(mine, others):
    vm = pl.BlockSpec(memory_space=VMEM)
    return pl.pallas_call(
        sum_kernel,
        in_specs=[vm] * 4,
        out_specs=vm,
        out_shape=jax.ShapeDtypeStruct(mine.shape, BF),
        compiler_params=params(),
        name="add_up",
    )(mine, *others)


def on_device(tokens, w_query, w_key, w_value, q_gain, k_gain, doc_lengths, w_out):
    tok, part = tokens.shape
    head = q_gain.shape[0]
    seqs, tps = lax.axis_size("seq"), lax.axis_size("tp")
    ny = 4
    nz = seqs // ny
    nx = tps // 2
    my_seq = lax.axis_index("seq")

    def sibling(a):
        return lax.ppermute(a, "tp", [(i, i ^ 1) for i in range(tps)])

    def along_x(a, d):
        return lax.ppermute(
            a,
            "tp",
            [(i, (i // 2 + (d if i % 2 == 0 else -d)) % nx * 2 + i % 2) for i in range(tps)],
        )

    def along_y(a, d):
        return lax.ppermute(a, "seq", [(i, i // ny * ny + (i + d) % ny) for i in range(seqs)])

    def along_y(a, d):
        return lax.ppermute(a, "seq", [(i, i // ny * ny + (i + d) % ny) for i in range(seqs)])

    def along_z(a, d):
        return lax.ppermute(a, "seq", [(i, (i // ny + d) % nz * ny + i % ny) for i in range(seqs)])

    def swap_y(a, turned):
        pairs = []
        for s in range(seqs):
            for t in range(tps):
                y = s % ny
                other = y ^ 1 if t % 2 == turned else ny - 1 - y
                pairs.append((s * tps + t, (s // ny * ny + other) * tps + t))
        return lax.ppermute(a, ("seq", "tp"), pairs)

    nq, nk = w_query.shape[1], w_key.shape[1]
    arrivals = [(0, 0), (0, 1), (-1, 0), (1, 0), (1, 1), (-1, 1), (2, 0), (2, 1)]
    plan = []
    for k, shard in enumerate(arrivals):
        plan += [(0, 0, part, shard, 0, k, 0, nq), (1, 0, part, shard, 0, k, nq, nk)]
        plan += [(2, 0, part, shard, 0, k, nq + nk, nk)]
    w_in, flag_in = stage(
        [w_query, w_key, w_value], tuple(plan), [(tps, part, nq + 2 * nk)], "stage_in"
    )
    token_index = my_seq * tok + jnp.arange(tok, dtype=jnp.int32)
    start = doc_tables(doc_lengths, token_index)
    cos, sin = rope_tables(token_index - start, head)
    start_col, index_col = start[:, None], token_index[:, None]

    own = tokens
    a1, a3, a2 = along_x(own, 1), along_x(own, nx - 1), along_x(own, 2)
    b0 = sibling(own)
    acc = project([own, b0], w_in, 0)
    a1, flags = after([flag_in], a1)
    b1 = sibling(a1)
    a3, acc, _ = after([], a3, acc)
    b3 = sibling(a3)
    a2, cos, sin, start_col, index_col, _ = after([], a2, cos, sin, start_col, index_col)
    b2 = sibling(a2)
    acc = project([a1, a3, b1, b3], w_in, 2, acc, flags=flags)
    queries, kv = project(
        [a2, b2], w_in, 6, acc, last=(cos, sin, q_gain[None, :], k_gain[None, :])
    )
    w_late, kv = lax.optimization_barrier((w_out, kv))
    cols = w_out.shape[1] // tps
    plan = [(0, 1, cols, (d, 0), 0, k, 0, cols) for k, d in enumerate((2, 1, -1, 0))]
    plan += [(0, 1, cols, (d, 1), 1, k, 0, cols) for k, d in enumerate((2, -1, 1, 0))]
    w_own, w_send, flag_out = stage(
        [w_late], tuple(plan), [(nx, w_out.shape[0], cols)] * 2, "stage_out"
    )

    attn = (start, queries, start_col, index_col)
    r0 = kv
    r1 = along_z(r0, 1)
    r1, staged = after([flag_out], r1)
    r2 = along_z(r1, 1)
    o, flag_a = attend(*attn, [(r0, [(0, 0)])])
    r2, first = after([flag_a], r2)
    r3 = along_z(r2, 1)
    r4 = along_z(r3, 1)
    s1, s2, s3 = swap_y(r1, 0), swap_y(r2, 0), swap_y(r3, 0)
    w_sib = sibling(w_send)
    got = hold(w_sib, cost=0)
    x_one, flag_1 = pack([r1, s1], [(0, 0), (1, 0)], tok, flags=staged)
    near_one = swap_y(x_one, 1)
    x_two, flag_2 = pack([r2, s2], [(0, 0), (1, 0)], tok, flags=[*first, hold(r3), got])
    near_two = swap_y(x_two, 1)
    x1, x2, x3, flag_m = mixes(r0, r4, flags=[hold(r4), flag_2])
    mixed = [(along_y((x1, x2, x3)[e - 1], e), [(None, e)]) for e in (1, 3, 2)]
    x_three, flag_3 = pack([r3, s3], [(0, 0), (1, 0)], tok, flags=[flag_m])
    near_three = swap_y(x_three, 1)
    o, flag_c = attend(
        *attn,
        [(r1, [(1, 0)]), (r2, [(2, 0)]), (s1, [(1, 1)]), (s2, [(2, 1)]), (near_one, [(1, 2), (1, 3)]), (r3, [(3, 0)])],
        o,
        flags=[flag_3],
    )
    o, flag_d = attend(
        *attn, [(near_two, [(2, 2), (2, 3)]), (s3, [(3, 1)]), (r4, [(4, 0)])], o
    )
    w_sib, flag_w = fetch(w_sib, [flag_d])
    attended, _ = attend(
        *attn,
        [(near_three, [(3, 2), (3, 3)]), *mixed],
        o,
        final=True,
        flags=[flag_w, hold(*[m for m, _ in mixed], flag_d, cost=2)],
    )

    attended_sib = sibling(attended)
    (p2,) = out_project((0,), (BF,), attended, attended_sib, w_own, w_sib)
    t2 = along_x(p2, 2)
    p1, p3 = out_project((1, 2), (BF, BF), attended, attended_sib, w_own, w_sib)
    t1 = along_x(p1, 1)
    t3 = along_x(p3, nx - 1)
    (mine,) = out_project((3,), (F32,), attended, attended_sib, w_own, w_sib)
    return add_up(mine, [t1, t2, t3])


def solution(mesh):
    return jax.shard_map(
        on_device,
        mesh=mesh,
        in_specs=(
            P("seq", "tp"),
            P(None, "tp"),
            P(None, "tp"),
            P(None, "tp"),
            P(),
            P(),
            P(),
            P("tp", None),
        ),
        out_specs=P("seq", "tp"),
        check_vma=False,
    )
```

```python
import functools
import math

import jax
import jax.numpy as jnp
from jax import lax
from jax.experimental import pallas as pl
from jax.experimental.pallas import tpu as pltpu
from jax.sharding import PartitionSpec as P

EPSILON = 1e-06
ROPE_THETA = 1000000.0
BF = jnp.bfloat16
F32 = jnp.float32
VMEM = pltpu.VMEM
MIB = 1024 * 1024


def params(limit=10):
    return pltpu.CompilerParams(vmem_limit_bytes=limit * MIB)


def doc_tables(doc_lengths, token_index):
    doc_ends = jnp.cumsum(doc_lengths)
    passed = (token_index[:, None] >= doc_ends[None, :]).astype(jnp.int32)
    return jnp.sum(passed * doc_lengths[None, :], axis=1)


def rope_tables(position, head_width):
    half = head_width // 2
    frequency = ROPE_THETA ** (-(jnp.arange(half, dtype=F32) * 2.0 / head_width))
    angles = position.astype(F32)[:, None] * frequency[None, :]
    cos, sin = jnp.cos(angles), jnp.sin(angles)
    return jnp.concatenate([cos, cos], axis=1), jnp.concatenate([-sin, sin], axis=1)


NX, NY = 4, 4


class Place:
    def __init__(self):
        seq, tp = lax.axis_index("seq"), lax.axis_index("tp")
        self.seq, self.z, self.y = seq, seq // NY, lax.rem(seq, NY)
        self.x, self.c = tp // 2, lax.rem(tp, 2)

        def flip(a):
            return a + 1 - 2 * lax.rem(a, 2)

        even = self.c == 0
        self.y1 = jnp.where(even, flip(self.y), NY - 1 - self.y)
        self.y2 = jnp.where(even, NY - 1 - self.y, flip(self.y))
        self.y3 = jnp.where(even, flip(self.y2), NY - 1 - self.y2)

    def chip(self, turn):
        return lax.rem(self.x + NX + turn * (1 - 2 * self.c), NX)

    def part(self, turn, other):
        return 2 * self.chip(turn) + (1 - self.c if other else self.c)

    def base(self, block, tok):
        back, who = block
        if back is None:
            wraps = self.y < who
            back, y = jnp.where(wraps, 4, 0), self.y - who + jnp.where(wraps, NY, 0)
        else:
            y = (self.y, self.y1, self.y2, self.y3)[who]
        return ((self.z - back) * NY + y) * tok


def stage_kernel(plan, sources, *refs):
    ins, rest = refs[:sources], refs[sources:]
    outs, flag, sem = rest[:-2], rest[-2], rest[-1]
    place = Place()
    copies = []
    for n, (src, axis, size, (turn, other), dst, row, col, cols) in enumerate(plan):
        cut = pl.ds(pl.multiple_of(place.part(turn, other) * size, size), size)
        view = ins[src].at[cut, :] if axis == 0 else ins[src].at[:, cut]
        copies.append(
            pltpu.make_async_copy(view, outs[dst].at[row, :, col : col + cols], sem.at[n])
        )
    for c in copies:
        c.start()
    flag[...] = jnp.zeros_like(flag)
    for c in copies:
        c.wait()


FLAG = (8, 128)


def fetch_kernel(src, *refs):
    out, flag, sem = refs[-3:]
    copy = pltpu.make_async_copy(src, out, sem)
    copy.start()
    flag[...] = jnp.zeros_like(flag)
    copy.wait()


def fetch(a, flags=()):
    vm = pl.BlockSpec(memory_space=VMEM)
    return pl.pallas_call(
        fetch_kernel,
        in_specs=[pl.BlockSpec(memory_space=pl.ANY)] * (1 + len(flags)),
        out_specs=[vm, vm],
        out_shape=[VMEM(a.shape, a.dtype), jax.ShapeDtypeStruct(FLAG, F32)],
        scratch_shapes=[pltpu.SemaphoreType.DMA],
        compiler_params=params(),
        name="fetch",
    )(a, *flags)


def stage(arrays, plan, shapes, name):
    vm = pl.BlockSpec(memory_space=VMEM)
    return pl.pallas_call(
        functools.partial(stage_kernel, plan, len(arrays)),
        in_specs=[pl.BlockSpec(memory_space=pltpu.HBM)] * len(arrays),
        out_specs=[vm] * (len(shapes) + 1),
        out_shape=[VMEM(shape, BF) for shape in shapes] + [jax.ShapeDtypeStruct(FLAG, F32)],
        scratch_shapes=[pltpu.SemaphoreType.DMA((len(plan),))],
        compiler_params=params(14),
        cost_estimate=pl.CostEstimate(
            flops=0, bytes_accessed=sum(4 * math.prod(shape) for shape in shapes), transcendentals=0
        ),
        name=name,
    )(*[pltpu.with_memory_space_constraint(a, pltpu.HBM) for a in arrays])


def after(flags, *arrays):
    out = lax.optimization_barrier((*arrays, *flags))
    return (*out[: len(arrays)], list(out[len(arrays) :]))


def hold_kernel(*refs):
    refs[-1][...] = jnp.zeros(FLAG, F32)


def hold(*arrays, cost=20):
    return pl.pallas_call(
        hold_kernel,
        in_specs=[pl.BlockSpec(memory_space=pl.ANY)] * len(arrays),
        out_specs=pl.BlockSpec(memory_space=VMEM),
        out_shape=jax.ShapeDtypeStruct(FLAG, F32),
        compiler_params=params(),
        cost_estimate=pl.CostEstimate(flops=cost * 10**9, bytes_accessed=4096, transcendentals=0),
        name="hold",
    )(*arrays)


def pack_kernel(pieces, tok, count, *refs):
    ins, out, flag = refs[:count], refs[-2], refs[-1]
    flag[...] = jnp.zeros_like(flag)
    for n, piece in enumerate(pieces):
        to = slice(n * tok, (n + 1) * tok)
        src, at = piece
        out[to, :] = ins[src][at * tok : (at + 1) * tok, :]


def pack(arrays, pieces, tok, flags=()):
    vm = pl.BlockSpec(memory_space=VMEM)
    count = len(arrays)
    return pl.pallas_call(
        functools.partial(pack_kernel, tuple(pieces), tok, count),
        in_specs=[vm] * count + [pl.BlockSpec(memory_space=pl.ANY)] * len(flags),
        out_specs=[vm, vm],
        out_shape=[
            VMEM((len(pieces) * tok, arrays[0].shape[1]), BF),
            jax.ShapeDtypeStruct(FLAG, F32),
        ],
        compiler_params=params(),
        name="pack",
    )(*arrays, *flags)


def mix_kernel(own, far, *refs):
    outs, flag = refs[-NY:-1], refs[-1]
    flag[...] = jnp.zeros_like(flag)
    place = Place()
    for e, out in enumerate(outs, 1):
        here = place.y + e < NY

        def put(src, out=out):
            out[...] = src[...]

        pl.when(here)(functools.partial(put, own))
        pl.when(jnp.logical_not(here))(functools.partial(put, far))


def mixes(own, far, flags=()):
    vm = pl.BlockSpec(memory_space=VMEM)
    return pl.pallas_call(
        mix_kernel,
        in_specs=[vm] * 2 + [pl.BlockSpec(memory_space=pl.ANY)] * len(flags),
        out_specs=[vm] * NY,
        out_shape=[VMEM(own.shape, BF)] * (NY - 1) + [jax.ShapeDtypeStruct(FLAG, F32)],
        compiler_params=params(),
        name="mixes",
    )(own, far, *flags)


def project_kernel(count, at, head, first, last, flags, *refs):
    chunks, w = refs[:count], refs[count]
    rest = refs[count + 1 :]
    outs = 2 if last else 1
    rest = rest[: len(rest) - flags - outs] + rest[len(rest) - outs :]
    total = None
    for k in range(count):
        prod = jnp.dot(chunks[k][...], w[at + k], preferred_element_type=F32)
        total = prod if total is None else total + prod
    if not first:
        total = total + rest[0][...]
        rest = rest[1:]
    if not last:
        rest[0][...] = total
        return
    cos_ref, sin_ref, qg, kg, q_out, kv_out = rest
    cos = cos_ref[...]
    sin = sin_ref[...]
    rows = total.shape[0]
    heads = total.shape[1] // head - 2

    def norm_rotate(x, gain):
        inv = lax.rsqrt(jnp.mean(x * x, axis=-1, keepdims=True) + EPSILON)
        x = x * inv * gain
        return (x * cos + pltpu.roll(x, head // 2, 1) * sin).astype(BF)

    kcol = heads * head
    kv_out[:, :head] = norm_rotate(total[:, kcol : kcol + head], kg[...])
    kv_out[:, head:] = total[:, kcol + head : kcol + 2 * head].astype(BF)
    for h in range(heads):
        q_out[h * rows : (h + 1) * rows, :] = norm_rotate(
            total[:, h * head : (h + 1) * head], qg[...]
        )


def project(chunks, w, at, acc=None, last=None, flags=()):
    count = len(chunks)
    rows, depth = chunks[0].shape
    width = w.shape[2]
    args = [*chunks, w] + ([] if acc is None else [acc]) + (list(last) if last else [])
    head = last[0].shape[1] if last else 128
    if last:
        heads = width // head - 2
        shape = [
            VMEM((heads * rows, head), BF),
            VMEM((rows, 2 * head), BF),
        ]
    else:
        shape = VMEM((rows, width), F32)
    vm = pl.BlockSpec(memory_space=VMEM)
    return pl.pallas_call(
        functools.partial(
            project_kernel, count, at, head, acc is None, last is not None, len(flags)
        ),
        in_specs=[vm] * len(args) + [pl.BlockSpec(memory_space=pl.ANY)] * len(flags),
        out_specs=[vm, vm] if last else vm,
        out_shape=shape,
        compiler_params=params(16),
        cost_estimate=pl.CostEstimate(
            flops=4 * rows * depth * count * width,
            bytes_accessed=2 * depth * count * width,
            transcendentals=0,
        ),
        name="project",
    )(*args, *flags)


def attend_kernel(layout, first, final, flags, start_s, *refs):
    n = len(layout)
    q_ref, start_ref, index_ref = refs[:3]
    kvs = refs[3 : 3 + n]
    rest = refs[3 + n :]
    if first:
        out, flag, acc = rest[flags:]
    else:
        acc_in = rest[0]
        out, flag, acc = rest[1 + flags :]
    flag[...] = jnp.zeros_like(flag)
    rows, head = q_ref.shape
    tok = start_ref.shape[0]
    heads = rows // tok
    scale = math.log2(math.e) / math.sqrt(head)
    if not final:
        acc = out
    acc[...] = jnp.zeros_like(acc) if first else acc_in[...]
    place = Place()
    own = place.seq * tok
    least = start_s[0]
    ones = jnp.ones((tok, head), BF)

    def unit(kv, bases):
        for j, base in enumerate(bases):
            at = slice(j * tok, (j + 1) * tok)
            keys = kv[at, :head]
            values = jnp.concatenate([kv[at, head:], ones], axis=1)
            col = base + lax.broadcasted_iota(jnp.int32, (tok, tok), 1)
            keep = (col >= start_ref[...]) & (col <= index_ref[...])
            for h in range(heads):
                part = slice(h * tok, (h + 1) * tok)
                s = lax.dot_general(
                    q_ref[part, :], keys, (((1,), (1,)), ((), ())), preferred_element_type=F32
                )
                p = jnp.where(keep, jnp.exp2(s * scale), 0.0).astype(BF)
                acc[part, :] += jnp.dot(p, values, preferred_element_type=F32)

    for kv, blocks in zip(kvs, layout):
        bases = [place.base(block, tok) for block in blocks]
        if blocks[0] == (0, 0):
            unit(kv, bases)
            continue
        needed = functools.reduce(
            jnp.logical_or, [(base + tok > least) & (base <= own) for base in bases]
        )
        pl.when(needed)(functools.partial(unit, kv, bases))
    if final:
        for h in range(heads):
            part = slice(h * tok, (h + 1) * tok)
            out[:, h * head : (h + 1) * head] = (acc[part, :head] / acc[part, head:]).astype(BF)


def attend(start, queries, start_col, index_col, pieces, acc=None, final=False, flags=()):
    rows, head = queries.shape
    tok = start_col.shape[0]
    kvs = [kv for kv, _ in pieces]
    layout = tuple(tuple(blocks) for _, blocks in pieces)
    first = acc is None
    args = [queries, start_col, index_col, *kvs] + ([] if first else [acc])
    if final:
        shape = VMEM((tok, rows // tok * head), BF)
    else:
        shape = VMEM((rows, 2 * head), F32)
    blocks = sum(len(blocks) for blocks in layout)
    vm = pl.BlockSpec(memory_space=VMEM)
    return pl.pallas_call(
        functools.partial(attend_kernel, layout, first, final, len(flags)),
        in_specs=[pl.BlockSpec(memory_space=pltpu.SMEM)]
        + [vm] * len(args)
        + [pl.BlockSpec(memory_space=pl.ANY)] * len(flags),
        out_specs=[vm, vm],
        out_shape=[shape, jax.ShapeDtypeStruct(FLAG, F32)],
        scratch_shapes=[pltpu.VMEM((rows, 2 * head), F32)],
        compiler_params=params(),
        cost_estimate=pl.CostEstimate(
            flops=blocks * rows * tok * head * 8,
            bytes_accessed=rows * head * 16,
            transcendentals=blocks * rows * tok,
        ),
        name="attend",
    )(start, *args, *flags)


def out_kernel(targets, a_ref, b_ref, wa, wb, *outs):
    for n, (target, out) in enumerate(zip(targets, outs)):
        s = jnp.dot(a_ref[...], wa[target], preferred_element_type=F32)
        s += jnp.dot(b_ref[...], wb[target], preferred_element_type=F32)
        out[...] = s.astype(out.dtype)


def out_project(targets, kinds, a, b, w_own, w_sib):
    rows, depth = a.shape
    cols = w_own.shape[2]
    vm = pl.BlockSpec(memory_space=VMEM)
    return pl.pallas_call(
        functools.partial(out_kernel, targets),
        in_specs=[vm] * 4,
        out_specs=[vm] * len(targets),
        out_shape=[VMEM((rows, cols), kind) for kind in kinds],
        compiler_params=params(),
        cost_estimate=pl.CostEstimate(
            flops=4 * rows * depth * cols * len(targets),
            bytes_accessed=4 * depth * cols * len(targets),
            transcendentals=0,
        ),
        name="out_project",
    )(a, b, w_own, w_sib)


def sum_kernel(mine, a, b, c, out):
    out[...] = (mine[...] + a[...].astype(F32) + b[...].astype(F32) + c[...].astype(F32)).astype(
        out.dtype
    )


def add_up(mine, others):
    vm = pl.BlockSpec(memory_space=VMEM)
    return pl.pallas_call(
        sum_kernel,
        in_specs=[vm] * 4,
        out_specs=vm,
        out_shape=jax.ShapeDtypeStruct(mine.shape, BF),
        compiler_params=params(),
        name="add_up",
    )(mine, *others)


def on_device(tokens, w_query, w_key, w_value, q_gain, k_gain, doc_lengths, w_out):
    tok, part = tokens.shape
    head = q_gain.shape[0]
    seqs, tps = lax.axis_size("seq"), lax.axis_size("tp")
    ny = 4
    nz = seqs // ny
    nx = tps // 2
    my_seq = lax.axis_index("seq")

    def sibling(a):
        return lax.ppermute(a, "tp", [(i, i ^ 1) for i in range(tps)])

    def along_x(a, d):
        return lax.ppermute(
            a,
            "tp",
            [(i, (i // 2 + (d if i % 2 == 0 else -d)) % nx * 2 + i % 2) for i in range(tps)],
        )

    def along_y(a, d):
        return lax.ppermute(a, "seq", [(i, i // ny * ny + (i + d) % ny) for i in range(seqs)])

    def along_y(a, d):
        return lax.ppermute(a, "seq", [(i, i // ny * ny + (i + d) % ny) for i in range(seqs)])

    def along_z(a, d):
        return lax.ppermute(a, "seq", [(i, (i // ny + d) % nz * ny + i % ny) for i in range(seqs)])

    def swap_y(a, turned):
        pairs = []
        for s in range(seqs):
            for t in range(tps):
                y = s % ny
                other = y ^ 1 if t % 2 == turned else ny - 1 - y
                pairs.append((s * tps + t, (s // ny * ny + other) * tps + t))
        return lax.ppermute(a, ("seq", "tp"), pairs)

    nq, nk = w_query.shape[1], w_key.shape[1]
    arrivals = [(0, 0), (0, 1), (-1, 0), (1, 0), (1, 1), (-1, 1), (2, 0), (2, 1)]
    plan = []
    for k, shard in enumerate(arrivals):
        plan += [(0, 0, part, shard, 0, k, 0, nq), (1, 0, part, shard, 0, k, nq, nk)]
        plan += [(2, 0, part, shard, 0, k, nq + nk, nk)]
    w_in, flag_in = stage(
        [w_query, w_key, w_value], tuple(plan), [(tps, part, nq + 2 * nk)], "stage_in"
    )
    token_index = my_seq * tok + jnp.arange(tok, dtype=jnp.int32)
    start = doc_tables(doc_lengths, token_index)
    cos, sin = rope_tables(token_index - start, head)
    start_col, index_col = start[:, None], token_index[:, None]

    own = tokens
    a1, a3, a2 = along_x(own, 1), along_x(own, nx - 1), along_x(own, 2)
    b0 = sibling(own)
    acc = project([own, b0], w_in, 0)
    a1, flags = after([flag_in], a1)
    b1 = sibling(a1)
    a3, acc, _ = after([], a3, acc)
    b3 = sibling(a3)
    a2, cos, sin, start_col, index_col, _ = after([], a2, cos, sin, start_col, index_col)
    b2 = sibling(a2)
    acc = project([a1, a3, b1, b3], w_in, 2, acc, flags=flags)
    queries, kv = project(
        [a2, b2], w_in, 6, acc, last=(cos, sin, q_gain[None, :], k_gain[None, :])
    )
    w_late, kv = lax.optimization_barrier((w_out, kv))
    cols = w_out.shape[1] // tps
    plan = [(0, 1, cols, (d, 0), 0, k, 0, cols) for k, d in enumerate((2, 1, -1, 0))]
    plan += [(0, 1, cols, (d, 1), 1, k, 0, cols) for k, d in enumerate((2, -1, 1, 0))]
    w_own, w_send, flag_out = stage(
        [w_late], tuple(plan), [(nx, w_out.shape[0], cols)] * 2, "stage_out"
    )

    attn = (start, queries, start_col, index_col)
    r0 = kv
    r1 = along_z(r0, 1)
    r1, staged = after([flag_out], r1)
    r2 = along_z(r1, 1)
    o, flag_a = attend(*attn, [(r0, [(0, 0)])])
    r2, first = after([flag_a], r2)
    r3 = along_z(r2, 1)
    r4 = along_z(r3, 1)
    s1, s2, s3 = swap_y(r1, 0), swap_y(r2, 0), swap_y(r3, 0)
    w_sib = sibling(w_send)
    got = hold(w_sib, cost=0)
    x_one, flag_1 = pack([r1, s1], [(0, 0), (1, 0)], tok, flags=staged)
    near_one = swap_y(x_one, 1)
    x_two, flag_2 = pack([r2, s2], [(0, 0), (1, 0)], tok, flags=[*first, hold(r3), got])
    near_two = swap_y(x_two, 1)
    x1, x2, x3, flag_m = mixes(r0, r4, flags=[hold(r4), flag_2])
    mixed = [(along_y((x1, x2, x3)[e - 1], e), [(None, e)]) for e in (1, 3, 2)]
    x_three, flag_3 = pack([r3, s3], [(0, 0), (1, 0)], tok, flags=[flag_m])
    near_three = swap_y(x_three, 1)
    o, flag_c = attend(
        *attn,
        [(r1, [(1, 0)]), (r2, [(2, 0)]), (s1, [(1, 1)]), (s2, [(2, 1)]), (near_one, [(1, 2), (1, 3)]), (r3, [(3, 0)])],
        o,
        flags=[flag_3],
    )
    o, flag_d = attend(
        *attn, [(near_two, [(2, 2), (2, 3)]), (s3, [(3, 1)]), (r4, [(4, 0)])], o
    )
    w_sib, flag_w = fetch(w_sib, [flag_d])
    attended, _ = attend(
        *attn,
        [(near_three, [(3, 2), (3, 3)]), *mixed],
        o,
        final=True,
        flags=[flag_w, hold(*[m for m, _ in mixed], flag_d, cost=2)],
    )

    attended_sib = sibling(attended)
    (p2,) = out_project((0,), (BF,), attended, attended_sib, w_own, w_sib)
    t2 = along_x(p2, 2)
    p1, p3 = out_project((1, 2), (BF, BF), attended, attended_sib, w_own, w_sib)
    t1 = along_x(p1, 1)
    t3 = along_x(p3, nx - 1)
    (mine,) = out_project((3,), (F32,), attended, attended_sib, w_own, w_sib)
    return add_up(mine, [t1, t2, t3])


def solution(mesh):
    return jax.shard_map(
        on_device,
        mesh=mesh,
        in_specs=(
            P("seq", "tp"),
            P(None, "tp"),
            P(None, "tp"),
            P(None, "tp"),
            P(),
            P(),
            P(),
            P("tp", None),
        ),
        out_specs=P("seq", "tp"),
        check_vma=False,
    )
```
